128 devices in a mesh: lon: 16 (over y, x_lo, core), lat: 8 (over z, x_hi).
Axes of the slice: x: 4 (x_hi: 2, x_lo: 2; x = x_hi * 2 + x_lo), y: 4, z: 4, core: 2. Of those that a mesh axis runs over, the one named last changes fastest.
Arguments:
- tokens: bfloat16 [4, 384, 48, 512], P(None, 'lon', 'lat'), may hold values from -6 to 6
- cotangent: bfloat16 [4, 192, 24, 1024], P(None, 'lon', 'lat'), may hold values from -6 to 6
- fine_qkv: bfloat16 [512, 1536], replicated, may hold values from -3 to 3
- fine_out: bfloat16 [512, 512], replicated, may hold values from -0.25 to 0.25
- merge_weight: bfloat16 [2048, 1024], replicated, may hold values from -0.125 to 0.125
- coarse_qkv: bfloat16 [1024, 3072], replicated, may hold values from -3 to 3
- coarse_out: bfloat16 [1024, 1024], replicated, may hold values from -0.1875 to 0.1875
Outputs:
- coarse: bfloat16 [4, 192, 24, 1024], P(None, 'lon', 'lat')
- d_tokens: bfloat16 [4, 384, 48, 512], P(None, 'lon', 'lat')
- grad_fine_qkv: float32 [512, 1536], P(('lon', 'lat'))
- grad_fine_out: float32 [512, 512], P(('lon', 'lat'))
- grad_merge: float32 [2048, 1024], P(('lon', 'lat'))
- grad_coarse_qkv: float32 [1024, 3072], P(('lon', 'lat'))
- grad_coarse_out: float32 [1024, 1024], P(('lon', 'lat'))
The draws below stay inside these ranges and needn't reach their ends.
All inputs are finite; a program needn't handle non-finite values.
Results may differ from the reference program's by a relative error of at most 0.03.
Values may be sent and summed in bfloat16 or wider, within the bound.
No kernel may reach another device: no remote copies, remote signals or barrier semaphores. Data moves between devices by JAX's collectives and lax.ppermute only.
A program may use at most 128 MiB of HBM per device.

```python
import jax
import jax.numpy as jnp
from jax import lax

D = 512
D2 = 1024
HEADS = 8
HEADS2 = 16
LEV = 4
WIN_LEV = 2
WIN_LON = 12
WIN_LAT = 6
SHIFT = 6
NLON = 384
NLAT = 48


def base_projection(key, fan_in, channels):
    normal_vals = jax.random.normal(key, (fan_in, 3 * channels), jnp.float32)
    return jnp.clip(normal_vals, -4.0, 4.0) * fan_in ** (-0.5)


def draw_fine_qkv(key, part):
    key = jax.random.fold_in(key, 11)
    base = base_projection(key, D, D)
    return base.astype(jnp.bfloat16)


def draw_coarse_qkv(key, part):
    key = jax.random.fold_in(key, 12)
    base = base_projection(key, D2, D2)
    return base.astype(jnp.bfloat16)


def steps_of(stream_key, dims, split, least, largest):
    level, own = 1.0, jax.random.fold_in(stream_key, 6)
    for dim, parts in split:
        steps = jnp.exp(jax.random.uniform(jax.random.fold_in(own, dim), (parts,), jnp.float32, least / len(split), largest / len(split)))
        level = level * jnp.repeat(steps, dims[dim] // parts).reshape([-1 if axis == dim else 1 for axis in range(len(dims))])
    return level


def scatter_about(key, extent, deviation, limit, cuts=(), dtype=jnp.bfloat16):
    factor_of = steps_of(key, extent, cuts, -0.22, 0.18) if cuts else 1.0
    array = jax.random.normal(key, extent, jnp.float32) * deviation * factor_of
    return jnp.minimum(jnp.maximum(array, -limit), limit).astype(dtype)


def setup_inputs(seed: int = 0) -> dict:
    arg_keys = jax.random.split(jax.random.key(seed), 8)
    tokens = scatter_about(arg_keys[0], (LEV, NLON, NLAT, D), 1.0, 6.0, ((1, 16), (2, 8)))
    cotangent = scatter_about(arg_keys[1], (LEV, NLON // 2, NLAT // 2, D2), 1.0, 6.0, ((1, 16), (2, 8)))
    fine_qkv = draw_fine_qkv(jax.random.fold_in(arg_keys[7], 71), 0)
    fine_out = scatter_about(arg_keys[3], (D, D), D ** -0.5, 0.25)
    merge_weight = scatter_about(arg_keys[4], (4 * D, D2), (4 * D) ** -0.5, 0.125)
    coarse_qkv = draw_coarse_qkv(jax.random.fold_in(arg_keys[7], 71), 0)
    coarse_out = scatter_about(arg_keys[6], (D2, D2), D2 ** -0.5, 0.1875)
    return dict(tokens=tokens, cotangent=cotangent, fine_qkv=fine_qkv, fine_out=fine_out, merge_weight=merge_weight, coarse_qkv=coarse_qkv, coarse_out=coarse_out)


NORM_EPS = 1e-05

def to_half(tensor):
    return lax.optimization_barrier(tensor.astype(jnp.bfloat16))

def layer_norm(vector_in):
    mean_val = lax.optimization_barrier(jnp.mean(vector_in, axis=-1, keepdims=True))
    centred = vector_in - mean_val
    variance = lax.optimization_barrier(jnp.mean(centred * centred, axis=-1, keepdims=True))
    return centred * lax.rsqrt(variance + NORM_EPS)

def norm_back(vector_in, upstream):
    return jax.vjp(layer_norm, vector_in)[1](upstream)[0]

def to_windows(grid_vals, lon_span, lat_span):
    levels, columns, latitudes, channels = grid_vals.shape
    blocks = grid_vals.reshape(levels // WIN_LEV, WIN_LEV, columns // lon_span, lon_span, latitudes // lat_span, lat_span, channels)
    blocks = blocks.transpose(0, 2, 4, 1, 3, 5, 6)
    return blocks.reshape(-1, WIN_LEV * lon_span * lat_span, channels)

def from_windows(windows, levels, columns, latitudes, lon_span, lat_span):
    channels = windows.shape[-1]
    blocks = windows.reshape(levels // WIN_LEV, columns // lon_span, latitudes // lat_span, WIN_LEV, lon_span, lat_span, channels)
    return blocks.transpose(0, 3, 1, 4, 2, 5, 6).reshape(levels, columns, latitudes, channels)

def split_heads(tensor, heads):
    return tensor.reshape(tensor.shape[0], tensor.shape[1], heads, tensor.shape[2] // heads).astype(jnp.float32)

def attend(queries, key_rows, value_rows, heads):
    scores = jnp.einsum('bqhd,bkhd->bhqk', split_heads(queries, heads), split_heads(key_rows, heads))
    attn_probs = jax.nn.softmax(scores, axis=-1)
    attn_weights = to_half(attn_probs).astype(jnp.float32)
    context = jnp.einsum('bhqk,bkhd->bqhd', attn_weights, split_heads(value_rows, heads))
    return (to_half(context.reshape(queries.shape)), attn_probs)

def attend_back(queries, key_rows, value_rows, attn_probs, d_context, heads):
    query_heads = split_heads(queries, heads)
    key_heads = split_heads(key_rows, heads)
    value_heads = split_heads(value_rows, heads)
    d_ctx_heads = split_heads(d_context, heads)
    attn_weights = to_half(attn_probs).astype(jnp.float32)
    d_weights = jnp.einsum('bqhd,bkhd->bhqk', d_ctx_heads, value_heads)
    d_values = jnp.einsum('bhqk,bqhd->bkhd', attn_weights, d_ctx_heads)
    d_scores = attn_probs * (d_weights - lax.optimization_barrier(jnp.sum(d_weights * attn_probs, axis=-1, keepdims=True)))
    d_half = to_half(d_scores).astype(jnp.float32)
    d_queries = jnp.einsum('bhqk,bkhd->bqhd', d_half, key_heads)
    d_keys = jnp.einsum('bhqk,bqhd->bkhd', d_half, query_heads)
    return (d_queries.reshape(queries.shape), d_keys.reshape(key_rows.shape), d_values.reshape(value_rows.shape))

def block_forward(windows, w_qkv, w_out, heads):
    channels = windows.shape[-1]
    query_scale = (channels // heads) ** (-0.5)
    normed = to_half(layer_norm(windows.astype(jnp.float32)))
    qkv = jnp.dot(normed, w_qkv, preferred_element_type=jnp.float32)
    queries = to_half(qkv[..., :channels] * query_scale)
    key_rows = to_half(qkv[..., channels:2 * channels])
    value_rows = to_half(qkv[..., 2 * channels:])
    context, attn_probs = attend(queries, key_rows, value_rows, heads)
    projected = jnp.dot(context, w_out, preferred_element_type=jnp.float32)
    result = to_half(windows.astype(jnp.float32) + projected)
    return (result, (normed, queries, key_rows, value_rows, attn_probs, context))

def block_backward(windows, stash, d_result, w_qkv, w_out, heads):
    normed, queries, key_rows, value_rows, attn_probs, context = stash
    channels = windows.shape[-1]
    query_scale = (channels // heads) ** (-0.5)
    grad_out = jnp.dot(context.reshape(-1, channels).T, d_result.reshape(-1, channels), preferred_element_type=jnp.float32)
    d_context = to_half(jnp.dot(d_result, w_out.T, preferred_element_type=jnp.float32))
    d_queries, d_keys, d_values = attend_back(queries, key_rows, value_rows, attn_probs, d_context, heads)
    d_qkv = to_half(jnp.concatenate([d_queries * query_scale, d_keys, d_values], axis=-1))
    grad_qkv = jnp.dot(normed.reshape(-1, channels).T, d_qkv.reshape(-1, 3 * channels), preferred_element_type=jnp.float32)
    d_normed = to_half(jnp.dot(d_qkv, w_qkv.T, preferred_element_type=jnp.float32))
    d_windows = to_half(d_result.astype(jnp.float32) + norm_back(windows.astype(jnp.float32), d_normed.astype(jnp.float32)))
    return (d_windows, grad_qkv, grad_out)

def merge_forward(fine_grid, w_merge):
    levels, columns, latitudes, channels = fine_grid.shape
    stacked = fine_grid.reshape(levels, columns // 2, 2, latitudes // 2, 2, channels)
    stacked = stacked.transpose(0, 1, 3, 2, 4, 5).reshape(levels, columns // 2, latitudes // 2, 4 * channels)
    normed = to_half(layer_norm(stacked.astype(jnp.float32)))
    merged = to_half(jnp.dot(normed, w_merge, preferred_element_type=jnp.float32))
    return (merged, stacked, normed)

def merge_backward(stacked, normed, d_merged, w_merge, channels):
    wide_channels = d_merged.shape[-1]
    grad_merge = jnp.dot(normed.reshape(-1, 4 * channels).T, d_merged.reshape(-1, wide_channels), preferred_element_type=jnp.float32)
    d_normed = to_half(jnp.dot(d_merged, w_merge.T, preferred_element_type=jnp.float32))
    d_stacked = to_half(norm_back(stacked.astype(jnp.float32), d_normed.astype(jnp.float32)))
    levels = d_stacked.shape[0]
    half_cols = d_stacked.shape[1]
    half_lats = d_stacked.shape[2]
    d_fine = d_stacked.reshape(levels, half_cols, half_lats, 2, 2, channels).transpose(0, 1, 3, 2, 4, 5)
    return (d_fine.reshape(levels, 2 * half_cols, 2 * half_lats, channels), grad_merge)

def window_scan(windows, d_results, w_qkv, w_out, heads, per_group):
    number, tokens_win, channels = windows.shape

    def scan_step(running, pair_item):
        block_wins, block_grads = pair_item
        result, stash = block_forward(block_wins, w_qkv, w_out, heads)
        d_block, grad_qkv, grad_out = block_backward(block_wins, stash, block_grads, w_qkv, w_out, heads)
        return ((running[0] + grad_qkv, running[1] + grad_out), (result, d_block))
    initial = (jnp.zeros(w_qkv.shape, jnp.float32), jnp.zeros(w_out.shape, jnp.float32))
    grouped = (windows.reshape(-1, per_group, tokens_win, channels), d_results.reshape(-1, per_group, tokens_win, channels))
    totals, outputs = lax.scan(scan_step, initial, grouped)
    return (outputs[0].reshape(number, tokens_win, channels), outputs[1].reshape(number, tokens_win, channels), totals[0], totals[1])

def reference(tokens, cotangent, fine_qkv, fine_out, merge_weight, coarse_qkv, coarse_out):
    levels, columns, latitudes, channels = tokens.shape
    shifted = jnp.roll(tokens, -SHIFT, axis=1)
    fine_windows = to_windows(shifted, WIN_LON, WIN_LAT)
    per_group = latitudes // WIN_LAT
    grouped = fine_windows.reshape(-1, per_group, fine_windows.shape[1], channels)
    fine_results = lax.map(lambda block_wins: block_forward(block_wins, fine_qkv, fine_out, HEADS)[0], grouped)
    fine_shifted_out = from_windows(fine_results.reshape(fine_windows.shape), levels, columns, latitudes, WIN_LON, WIN_LAT)
    fine_state = jnp.roll(fine_shifted_out, SHIFT, axis=1)
    merged, stacked, merge_normed = merge_forward(fine_state, merge_weight)
    coarse_windows = to_windows(merged, WIN_LON, WIN_LAT)
    cot_windows = to_windows(cotangent, WIN_LON, WIN_LAT)
    coarse_res, d_coarse_wins, grad_cqkv, grad_cout = window_scan(coarse_windows, cot_windows, coarse_qkv, coarse_out, HEADS2, latitudes // 2 // WIN_LAT)
    coarse = from_windows(coarse_res, levels, columns // 2, latitudes // 2, WIN_LON, WIN_LAT)
    d_merged = from_windows(d_coarse_wins, levels, columns // 2, latitudes // 2, WIN_LON, WIN_LAT)
    d_fine_state, grad_merge = merge_backward(stacked, merge_normed, d_merged, merge_weight, channels)
    d_shifted = jnp.roll(d_fine_state, -SHIFT, axis=1)
    d_shift_wins = to_windows(d_shifted, WIN_LON, WIN_LAT)
    unused_res, d_fine_wins, grad_fqkv, grad_fout = window_scan(fine_windows, d_shift_wins, fine_qkv, fine_out, HEADS, per_group)
    d_tokens = jnp.roll(from_windows(d_fine_wins, levels, columns, latitudes, WIN_LON, WIN_LAT), SHIFT, axis=1)
    grad_factor = (levels * (columns // 2) * (latitudes // 2)) ** (-0.5)
    return (coarse, d_tokens, grad_fqkv * grad_factor, grad_fout * grad_factor, grad_merge * grad_factor, grad_cqkv * grad_factor, grad_cout * grad_factor)
```

```python
import functools

import jax
import jax.numpy as jnp
import numpy as np
from jax import lax
from jax.experimental import pallas as pl
from jax.experimental.pallas import tpu as pltpu
from jax.sharding import PartitionSpec as P

HEADS = 8
HEADS2 = 16
NORM_EPS = 1e-05
BF = jnp.bfloat16
F32 = jnp.float32
VMEM = pl.BlockSpec(memory_space=pltpu.VMEM)
MIB = 1024 * 1024


def fine_index(pair, quarter, level, lat, lon):
    return (pair * 4 + quarter) * 72 + level * 36 + lat * 6 + lon


def place_tokens():
    own = np.zeros((576, 576), np.float32)
    halo = np.zeros((576, 192), np.float32)
    for pair in range(2):
        for quarter in range(4):
            for level in range(2):
                for lat in range(6):
                    for lon in range(6):
                        row = fine_index(pair, quarter, level, lat, lon)
                        col = 6 * quarter + lon + 6
                        line = (2 * pair + level) * 6 + lat
                        if col < 24:
                            own[row, line * 24 + col] = 1
                        else:
                            halo[row, line * 8 + col - 24] = 1
    return own, halo


def place_stacked():
    body = np.zeros((576, 432), np.float32)
    tail = np.zeros((576, 144), np.float32)
    for a in range(2):
        for b in range(2):
            for pair in range(2):
                for level in range(2):
                    for i in range(12):
                        for j in range(3):
                            row = (a * 2 + b) * 144 + pair * 72 + level * 36 + i * 3 + j
                            quarter, lon, lat = i // 3, 2 * (i % 3) + a, 2 * j + b
                            inner = level * 36 + lat * 6 + lon
                            if quarter == 0:
                                tail[row, pair * 72 + inner] = 1
                            else:
                                body[row, pair * 216 + (quarter - 1) * 72 + inner] = 1
    return body, tail


def place_result():
    body = np.zeros((576, 432), np.float32)
    tail = np.zeros((576, 144), np.float32)
    for level in range(4):
        for lat in range(6):
            for lon in range(24):
                row = (level * 6 + lat) * 24 + lon
                inner = (level % 2) * 36 + lat * 6
                if lon < 6:
                    tail[row, (level // 2) * 72 + inner + lon] = 1
                else:
                    quarter = (lon - 6) // 6
                    body[row, (level // 2) * 216 + quarter * 72 + inner + lon % 6] = 1
    return body, tail


def dot(a, b):
    return lax.dot_general(a, b, (((1,), (0,)), ((), ())), preferred_element_type=F32)


def dot_nt(a, b):
    return lax.dot_general(a, b, (((1,), (1,)), ((), ())), preferred_element_type=F32)


def dot_tn(a, b):
    return lax.dot_general(a, b, (((0,), (0,)), ((), ())), preferred_element_type=F32)


def steps(count, body):
    lax.fori_loop(0, count, lambda i, carry: (body(i), carry)[1], 0)


def span(i, size):
    return pl.ds(pl.multiple_of(i * size, size), size)


def total(x):
    return jnp.sum(x, axis=-1, keepdims=True)


def norm_parts(parts):
    width = sum(p.shape[1] for p in parts)
    mean = sum(total(p) for p in parts) * (1.0 / width)
    centred = [p - mean for p in parts]
    rstd = lax.rsqrt(sum(total(c * c) for c in centred) * (1.0 / width) + NORM_EPS)
    return [c * rstd for c in centred], rstd


def norm_back(normed, rstd, upstream):
    width = sum(p.shape[1] for p in normed)
    first = sum(total(u) for u in upstream) * (1.0 / width)
    second = sum(total(u * n) for u, n in zip(upstream, normed)) * (1.0 / width)
    return [rstd * (u - first - n * second) for u, n in zip(upstream, normed)]


def half_masks(rows):
    lane = lax.broadcasted_iota(jnp.int32, (rows, 128), 1)
    low = lane < 64
    return low, jnp.where(low, 1.0, 0.0).astype(BF), jnp.where(low, 0.0, 1.0).astype(BF)


def two_heads(x, masks):
    return jnp.concatenate([x * masks[1], x * masks[2]], axis=0)


def one_row(x, masks):
    rows = x.shape[0] // 2
    return jnp.where(masks[0], x[:rows], x[rows:])


def softmax(scores):
    shifted = jnp.exp(scores - jnp.max(scores, axis=-1, keepdims=True))
    return shifted * (1.0 / total(shifted))


def attend_back(queries, keys, values, d_context, probs, weights, masks):
    d_weights = dot_nt(d_context, values)
    d_scores = (probs * (d_weights - total(d_weights * probs))).astype(BF)
    d_queries = one_row(dot(d_scores, keys), masks)
    d_keys = dot_tn(d_scores, queries)
    d_values = dot_tn(weights, d_context)
    return d_queries, d_keys, d_values


def axis_places():
    lon, lat = lax.axis_index("lon"), lax.axis_index("lat")
    return jnp.stack([lon >> 2, (lon >> 1) & 1, lon & 1, lat >> 1, lat & 1]).astype(jnp.int32)


def row_choice(place, rows, features, per_share, both_halves):
    r = lax.broadcasted_iota(jnp.int32, (rows, features), 0)
    col = lax.broadcasted_iota(jnp.int32, (rows, features), 1)
    low = r & (per_share - 1)
    r = r >> (per_share.bit_length() - 1)
    if both_halves:
        x_hi = (r & 1) ^ place[4]
        r = r >> 1
    else:
        x_hi = place[4]
    x_lo = (r & 1) ^ place[1]
    z = ((r >> 1) + place[3]) & 3
    core = ((r >> 3) & 1) ^ place[2]
    share = ((x_lo * 2 + core) * 8) + z * 2 + x_hi
    return jnp.where(share * per_share + low == col, 1.0, 0.0).astype(BF)


def fine_forward_kernel(
    tok, halo, put_own, put_halo, w_qkv, w_out, body, tail, x_out, qkv_out, ctx_out, prob_out
):
    x = dot(put_own[...], tok[...]) + dot(put_halo[...], halo[...])
    x_out[...] = x.astype(BF)
    (normed,), _ = norm_parts([x])
    normed = normed.astype(BF)
    for n in range(3):
        part = dot(normed, w_qkv[:, n * 512 : (n + 1) * 512])
        if n == 0:
            part = part * (512 // HEADS) ** (-0.5)
        qkv_out[:, n * 512 : (n + 1) * 512] = part.astype(BF)
    masks = half_masks(144)

    def window(w):
        rows = span(w, 144)
        for h in range(4):
            lanes = slice(h * 128, (h + 1) * 128)
            queries = two_heads(qkv_out[rows, lanes], masks)
            keys = qkv_out[rows, 512 + h * 128 : 512 + (h + 1) * 128]
            values = qkv_out[rows, 1024 + h * 128 : 1024 + (h + 1) * 128]
            weights = softmax(dot_nt(queries, keys)).astype(BF)
            prob_out[w * 4 + h] = weights
            ctx_out[rows, lanes] = one_row(dot(weights, values), masks).astype(BF)

    steps(4, window)
    result = x + dot(ctx_out[...], w_out[...])
    body[...] = jnp.concatenate([result[0:216], result[288:504]], axis=0).astype(BF)
    tail[...] = jnp.concatenate([result[216:288], result[504:576]], axis=0).astype(BF)


def interleave(own, far):
    return jnp.concatenate([own[:72], far[:72], own[72:], far[72:]], axis=0)


def own_rows(x):
    return jnp.concatenate([x[0:72], x[144:216]], axis=0)


def coarse_kernel(
    place_ref,
    body_own,
    tail_own,
    body_far,
    tail_far,
    put_body,
    put_tail,
    cot_own,
    cot_far,
    w_merge,
    w_qkv,
    w_out,
    coarse,
    d_merged_out,
    d_own_out,
    stacked_out,
    send,
    keep,
    merged_ref,
    normed_ref,
    qkv_ref,
    ctx_ref,
    cot_ref,
    d_ctx_ref,
    d_qkv_ref,
    left_qkv,
    left_out,
    factor,
):
    place = [place_ref[i] for i in range(5)]
    own = dot(put_body[...], body_own[...]) + dot(put_tail[...], tail_own[...])
    far = dot(put_body[...], body_far[...]) + dot(put_tail[...], tail_far[...])
    parts = [interleave(own[g * 144 : (g + 1) * 144], far[g * 144 : (g + 1) * 144]) for g in range(4)]
    for g in range(4):
        stacked_out[g] = parts[g].astype(BF)
    normed, _ = norm_parts(parts)
    merged = sum(dot(normed[g].astype(BF), w_merge[g * 512 : (g + 1) * 512, :]) for g in range(4))
    merged_ref[...] = merged.astype(BF)
    merged = merged_ref[...].astype(F32)
    (normed,), _ = norm_parts([merged])
    normed_ref[...] = normed.astype(BF)
    cot_ref[...] = interleave(cot_own[...].astype(F32), cot_far[...].astype(F32)).astype(BF)

    def project(n):
        part = dot(normed_ref[...], w_qkv[:, span(n, 512)])
        scale = jnp.where(n < 2, (1024 // HEADS2) ** (-0.5), 1.0)
        qkv_ref[:, span(n, 512)] = (part * scale).astype(BF)

    steps(6, project)

    def back_out(n):
        d_ctx_ref[:, span(n, 512)] = dot_nt(cot_ref[...], w_out[span(n, 512), :]).astype(BF)

    steps(2, back_out)
    masks = half_masks(144)

    def heads(h):
        for pair in range(2):
            rows = slice(pair * 144, (pair + 1) * 144)
            queries = two_heads(qkv_ref[rows, span(h, 128)], masks)
            keys = qkv_ref[rows, span(h + 8, 128)]
            values = qkv_ref[rows, span(h + 16, 128)]
            d_context = two_heads(d_ctx_ref[rows, span(h, 128)], masks)
            probs = softmax(dot_nt(queries, keys))
            weights = probs.astype(BF)
            ctx_ref[rows, span(h, 128)] = one_row(dot(weights, values), masks).astype(BF)
            d_queries, d_keys, d_values = attend_back(
                queries, keys, values, d_context, probs, weights, masks
            )
            d_qkv_ref[rows, span(h, 128)] = (d_queries * (1024 // HEADS2) ** (-0.5)).astype(BF)
            d_qkv_ref[rows, span(h + 8, 128)] = d_keys.astype(BF)
            d_qkv_ref[rows, span(h + 16, 128)] = d_values.astype(BF)

    steps(8, heads)

    choice = row_choice(place, 128, 256, 8, False)
    for y in range(4):
        lanes = span((place[0] + y) & 3, 256)
        block = dot_nt(choice, normed_ref[:, lanes]).astype(BF)
        other = dot_nt(choice, ctx_ref[:, lanes]).astype(BF)
        for cz in range(8):
            rows = slice((cz * 4 + y) * 16, (cz * 4 + y + 1) * 16)
            left_qkv[rows] = block[cz * 16 : (cz + 1) * 16]
            left_out[rows] = other[cz * 16 : (cz + 1) * 16]

    def grads_qkv(n):
        part = (dot(left_qkv[...], d_qkv_ref[:, span(n, 512)]) * factor).astype(BF)
        keep[:, span(n, 512)] = part[:256]
        send[:, span(n, 512)] = part[256:]

    steps(6, grads_qkv)

    def grads_out(n):
        part = (dot(left_out[...], cot_ref[:, span(n, 512)]) * factor).astype(BF)
        keep[:, span(n + 6, 512)] = part[:256]
        send[:, span(n + 6, 512)] = part[256:]

    steps(2, grads_out)

    projected = dot(ctx_ref[...], w_out[...])
    coarse[...] = own_rows(merged_ref[...].astype(F32) + projected).astype(BF)

    d_normed = jnp.zeros((288, 1024), F32)
    for n in range(3):
        d_normed = d_normed + dot_nt(
            d_qkv_ref[:, n * 1024 : (n + 1) * 1024], w_qkv[:, n * 1024 : (n + 1) * 1024]
        )
    d_normed = d_normed.astype(BF).astype(F32)
    (normed,), rstd = norm_parts([merged_ref[...].astype(F32)])
    (d_input,) = norm_back([normed], rstd, [d_normed])
    d_input = cot_ref[...].astype(F32) + d_input
    d_merged_out[...] = d_input.astype(BF)
    d_own_out[...] = own_rows(d_input).astype(BF)


def merge_back_kernel(
    place_ref,
    stacked,
    d_merged,
    d_own,
    put_body,
    put_tail,
    w_merge,
    d_body,
    d_tail,
    send,
    keep,
    normed_ref,
    d_stacked_ref,
    left,
    factor,
):
    place = [place_ref[i] for i in range(5)]
    normed, rstd = norm_parts([stacked[g].astype(F32) for g in range(4)])
    for g in range(4):
        normed_ref[g] = normed[g].astype(BF)
    upstream = []
    for g in range(4):
        part = dot_nt(d_own[...], w_merge[g * 512 : (g + 1) * 512, :])
        upstream.append(part.astype(BF).astype(F32))
    own = norm_back([own_rows(n) for n in normed], own_rows(rstd), upstream)
    for g in range(4):
        d_stacked_ref[g * 144 : (g + 1) * 144, :] = own[g].astype(BF)
    d_tail[...] = dot(put_tail[...], d_stacked_ref[...]).astype(BF)
    d_body[...] = dot(put_body[...], d_stacked_ref[...]).astype(BF)

    choice = row_choice(place, 256, 512, 16, False)
    for y in range(4):
        block = dot_nt(choice, normed_ref[(place[0] + y) & 3]).astype(BF)
        for cz in range(8):
            left[(cz * 4 + y) * 32 : (cz * 4 + y + 1) * 32] = block[cz * 32 : (cz + 1) * 32]
    for n in range(2):
        lanes = slice(n * 512, (n + 1) * 512)
        part = (dot(left[...], d_merged[:, lanes]) * factor).astype(BF)
        keep[:, lanes] = part[:512]
        send[:, lanes] = part[512:]


def fine_back_kernel(
    place_ref,
    d_body,
    d_tail,
    x_in,
    qkv,
    ctx,
    prob,
    w_qkv,
    w_out,
    body,
    tail,
    send,
    keep,
    normed_ref,
    d_res_ref,
    d_ctx_ref,
    d_qkv_ref,
    left_qkv,
    left_out,
    factor,
):
    place = [place_ref[i] for i in range(5)]
    d_own, d_far = d_body[...].astype(F32), d_tail[...].astype(F32)
    d_result = jnp.concatenate([d_own[:216], d_far[:72], d_own[216:], d_far[72:]], axis=0)
    d_res_ref[...] = d_result.astype(BF)
    d_ctx_ref[...] = dot_nt(d_res_ref[...], w_out[...]).astype(BF)
    (normed,), rstd = norm_parts([x_in[...].astype(F32)])
    normed_ref[...] = normed.astype(BF)
    masks = half_masks(144)

    def window(w):
        rows = span(w, 144)
        for h in range(4):
            lanes = slice(h * 128, (h + 1) * 128)
            queries = two_heads(qkv[rows, lanes], masks)
            keys = qkv[rows, 512 + h * 128 : 512 + (h + 1) * 128]
            values = qkv[rows, 1024 + h * 128 : 1024 + (h + 1) * 128]
            d_context = two_heads(d_ctx_ref[rows, lanes], masks)
            weights = prob[w * 4 + h]
            d_queries, d_keys, d_values = attend_back(
                queries, keys, values, d_context, weights.astype(F32), weights, masks
            )
            d_qkv_ref[rows, lanes] = (d_queries * (512 // HEADS) ** (-0.5)).astype(BF)
            d_qkv_ref[rows, 512 + h * 128 : 512 + (h + 1) * 128] = d_keys.astype(BF)
            d_qkv_ref[rows, 1024 + h * 128 : 1024 + (h + 1) * 128] = d_values.astype(BF)

    steps(4, window)

    choice = row_choice(place, 128, 128, 4, True)
    for y in range(4):
        lanes = span((place[0] + y) & 3, 128)
        block = dot_nt(choice, normed_ref[:, lanes]).astype(BF)
        other = dot_nt(choice, ctx[:, lanes]).astype(BF)
        for cz in range(8):
            rows = slice((cz * 4 + y) * 16, (cz * 4 + y + 1) * 16)
            left_qkv[rows] = block[cz * 16 : (cz + 1) * 16]
            left_out[rows] = other[cz * 16 : (cz + 1) * 16]

    def grads_qkv(n):
        part = (dot(left_qkv[...], d_qkv_ref[:, span(n, 512)]) * factor).astype(BF)
        keep[:, span(n, 512)] = part[:256]
        send[:, span(n, 512)] = part[256:]

    steps(3, grads_qkv)
    part = (dot(left_out[...], d_res_ref[...]) * factor).astype(BF)
    keep[:, 1536:] = part[:256]
    send[:, 1536:] = part[256:]

    d_normed = dot_nt(d_qkv_ref[...], w_qkv[...]).astype(BF).astype(F32)
    (d_input,) = norm_back([normed], rstd, [d_normed])
    d_input = d_res_ref[...].astype(F32) + d_input
    body[...] = jnp.concatenate([d_input[0:216], d_input[288:504]], axis=0).astype(BF)
    tail[...] = jnp.concatenate([d_input[216:288], d_input[504:576]], axis=0).astype(BF)


def place_result_kernel(body, tail, put_body, put_tail, out):
    out[...] = (dot(put_body[...], body[...]) + dot(put_tail[...], tail[...])).astype(BF)


def call(kernel, outs, scratch=(), scalars=0, limit=56):
    def run(*args):
        in_specs = [pl.BlockSpec(memory_space=pltpu.SMEM)] * scalars + [VMEM] * (len(args) - scalars)
        return pl.pallas_call(
            kernel,
            out_shape=[jax.ShapeDtypeStruct(shape, dtype) for shape, dtype in outs],
            in_specs=in_specs,
            out_specs=[VMEM] * len(outs),
            scratch_shapes=[pltpu.VMEM(shape, dtype) for shape, dtype in scratch],
            compiler_params=pltpu.CompilerParams(vmem_limit_bytes=limit * MIB),
        )(*args)

    return run


def route(move):
    pairs = []
    for source in range(128):
        lon, lat = divmod(source, 8)
        y, x_lo, core, z, x_hi = move(lon >> 2, (lon >> 1) & 1, lon & 1, lat >> 1, lat & 1)
        pairs.append((source, (((y & 3) * 2 + x_lo) * 2 + core) * 8 + (z & 3) * 2 + x_hi))
    return pairs


def send_core(x):
    return lax.ppermute(x, ("lon", "lat"), route(lambda y, xl, c, z, xh: (y, xl, 1 - c, z, xh)))


def send_z(x, d):
    return lax.ppermute(x, ("lon", "lat"), route(lambda y, xl, c, z, xh: (y, xl, c, z + d, xh)))


def send_y(x, d):
    return lax.ppermute(x, ("lon", "lat"), route(lambda y, xl, c, z, xh: (y + d, xl, c, z, xh)))


def send_x_lo(x):
    return lax.ppermute(x, ("lon", "lat"), route(lambda y, xl, c, z, xh: (y, 1 - xl, c, z, xh)))


def send_x_hi(x):
    return lax.ppermute(x, ("lon", "lat"), route(lambda y, xl, c, z, xh: (y, xl, c, z, 1 - xh)))


def send_lon(x, step, partner):
    pairs = []
    for lon in range(16):
        for lat in range(8):
            pairs.append((lon * 8 + lat, (lon + step) % 16 * 8 + (lat ^ partner)))
    return lax.ppermute(x, ("lon", "lat"), pairs)


def add_split_kernel(keep, got, *pieces):
    half = keep.shape[3] // 2
    for d in range(4):
        first = keep[d, :, :, :half].astype(F32) + got[d, :, :, :half].astype(F32)
        pieces[d][...] = first.astype(BF)
        last = keep[:, d, :, half:].astype(F32) + got[:, d, :, half:].astype(F32)
        pieces[4 + d][...] = last.astype(BF)


def add_four_kernel(*refs):
    sums = [sum(r[...].astype(F32) for r in refs[s * 4 : s * 4 + 4]).astype(BF) for s in range(2)]
    for s in range(2):
        for d in range(4):
            refs[8 + s * 4 + d][...] = sums[s][d]


def add_last_kernel(*refs):
    sums = [sum(r[...].astype(F32) for r in refs[s * 4 : s * 4 + 4]).astype(BF) for s in range(2)]
    both = jnp.concatenate(sums, axis=1)
    rows = both.shape[0] // 2
    refs[8][...] = both[:rows]
    refs[9][...] = both[rows:]


def spread_core(send, keep, rows, columns):
    return keep.reshape(4, 4, rows, columns), send_core(send).reshape(4, 4, rows, columns)


def reduce_first(keep, got):
    rows, columns = keep.shape[2:]
    pieces = call(add_split_kernel, [((4, rows, columns // 2), BF)] * 8)(keep, got)
    return (
        [pieces[0]] + [send_z(pieces[d], d) for d in (1, 2, 3)],
        [pieces[4]] + [send_y(pieces[4 + d], d) for d in (1, 2, 3)],
    )


def reduce_second(first, last):
    shape = first[0].shape[1:]
    pieces = call(add_four_kernel, [(shape, BF)] * 8)(*first, *last)
    return (
        [pieces[0]] + [send_y(pieces[d], d) for d in (1, 2, 3)],
        [pieces[4]] + [send_z(pieces[4 + d], d) for d in (1, 2, 3)],
    )


def reduce_third(first, last):
    rows, columns = first[0].shape
    keep, send = call(add_last_kernel, [((rows // 2, columns * 2), BF)] * 2)(*first, *last)
    return keep, send_x_lo(send)


def local(tokens, cotangent, fine_qkv, fine_out, merge_weight, coarse_qkv, coarse_out):
    factor = (144 * lax.axis_size("lon") * lax.axis_size("lat")) ** (-0.5)
    place = axis_places()
    put_own, put_halo = (jnp.asarray(a, BF) for a in place_tokens())
    stack_body, stack_tail = place_stacked()
    back_body, back_tail = (jnp.asarray(a, BF) for a in place_result())

    tok = tokens.transpose(0, 2, 1, 3)
    halo = send_lon(tok[:, :, :8], -1, 0).reshape(192, 512)
    cot_own = cotangent.reshape(144, 1024)
    cot_far = send_lon(cot_own, 0, 1)

    body, tail, x_fine, qkv_fine, ctx_fine, prob_fine = call(
        fine_forward_kernel,
        [
            ((432, 512), BF),
            ((144, 512), BF),
            ((576, 512), BF),
            ((576, 1536), BF),
            ((576, 512), BF),
            ((16, 288, 144), BF),
        ],
    )(tok.reshape(576, 512), halo, put_own, put_halo, fine_qkv, fine_out)
    tail_own = send_lon(tail, 1, 0)
    tail_far = send_lon(tail, 1, 1)
    body_far = send_lon(body, 0, 1)

    coarse, d_merged, d_merged_own, stacked, send_a, keep_a = call(
        functools.partial(coarse_kernel, factor=factor),
        [
            ((144, 1024), BF),
            ((288, 1024), BF),
            ((144, 1024), BF),
            ((4, 288, 512), BF),
            ((256, 4096), BF),
            ((256, 4096), BF),
        ],
        [
            ((288, 1024), BF),
            ((288, 1024), BF),
            ((288, 3072), BF),
            ((288, 1024), BF),
            ((288, 1024), BF),
            ((288, 1024), BF),
            ((288, 3072), BF),
            ((512, 288), BF),
            ((512, 288), BF),
        ],
        scalars=1,
    )(
        place,
        body,
        tail_own,
        body_far,
        tail_far,
        jnp.asarray(stack_body, BF),
        jnp.asarray(stack_tail, BF),
        cot_own,
        cot_far,
        merge_weight,
        coarse_qkv,
        coarse_out,
    )
    core_a = spread_core(send_a, keep_a, 16, 4096)

    d_body, d_tail, send_m, keep_m = call(
        functools.partial(merge_back_kernel, factor=factor),
        [((432, 512), BF), ((144, 512), BF), ((512, 1024), BF), ((512, 1024), BF)],
        [((4, 288, 512), BF), ((576, 512), BF), ((1024, 288), BF)],
        scalars=1,
    )(
        place,
        stacked,
        d_merged,
        d_merged_own,
        jnp.asarray(stack_body.T, BF),
        jnp.asarray(stack_tail.T, BF),
        merge_weight,
    )
    d_tail_east = send_lon(d_tail, -1, 0)
    core_m = spread_core(send_m, keep_m, 32, 1024)
    first_a = reduce_first(*core_a)
    first_m = reduce_first(*core_m)

    d_in_body, d_in_tail, send_f, keep_f = call(
        functools.partial(fine_back_kernel, factor=factor),
        [((432, 512), BF), ((144, 512), BF), ((256, 2048), BF), ((256, 2048), BF)],
        [
            ((576, 512), BF),
            ((576, 512), BF),
            ((576, 512), BF),
            ((576, 1536), BF),
            ((512, 576), BF),
            ((512, 576), BF),
        ],
        scalars=1,
    )(place, d_body, d_tail_east, x_fine, qkv_fine, ctx_fine, prob_fine, fine_qkv, fine_out)
    core_f = spread_core(send_f, keep_f, 16, 2048)
    d_in_west = send_lon(d_in_tail, 1, 0)
    second_a = reduce_second(*first_a)
    second_m = reduce_second(*first_m)
    first_f = reduce_first(*core_f)
    (d_tokens,) = call(place_result_kernel, [((576, 512), BF)])(
        d_in_body, d_in_west, back_body, back_tail
    )
    keep_a, got_a = reduce_third(*second_a)
    keep_m, got_m = reduce_third(*second_m)
    keep_f, got_f = reduce_third(*reduce_second(*first_f))
    share_a = keep_a.astype(F32) + got_a.astype(F32)
    share_m = keep_m.astype(F32) + got_m.astype(F32)
    share_f = (keep_f.astype(F32) + got_f.astype(F32)).reshape(2, 4, 2048)
    share_f = share_f[0] + send_x_hi(share_f[1].astype(BF)).astype(F32)
    return (
        coarse.reshape(4, 12, 3, 1024),
        d_tokens.reshape(4, 6, 24, 512).transpose(0, 2, 1, 3),
        share_f[:, :1536],
        share_f[:, 1536:],
        share_m,
        share_a[:, :3072],
        share_a[:, 3072:],
    )


def solution(mesh):
    grid_spec = P(None, "lon", "lat", None)
    rows_spec = P(("lon", "lat"), None)
    return jax.shard_map(
        local,
        mesh=mesh,
        in_specs=(grid_spec, grid_spec, P(), P(), P(), P(), P()),
        out_specs=(grid_spec, grid_spec) + (rows_spec,) * 5,
        check_vma=False,
    )
```

```python
import functools

import jax
import jax.numpy as jnp
import numpy as np
from jax import lax
from jax.experimental import pallas as pl
from jax.experimental.pallas import tpu as pltpu
from jax.sharding import PartitionSpec as P

HEADS = 8
HEADS2 = 16
NORM_EPS = 1e-05
BF = jnp.bfloat16
F32 = jnp.float32
VMEM = pl.BlockSpec(memory_space=pltpu.VMEM)
MIB = 1024 * 1024


def place_tokens():
    first = np.zeros((288, 576), np.float32)
    second = np.zeros((288, 576), np.float32)
    halo = np.zeros((288, 192), np.float32)
    for pair in range(2):
        for quarter in range(4):
            for level in range(2):
                for lat in range(6):
                    for lon in range(6):
                        row = pair * 144 + (quarter % 2) * 72 + level * 36 + lat * 6 + lon
                        col = 6 * quarter + lon + 6
                        line = (2 * pair + level) * 6 + lat
                        if col >= 24:
                            halo[row, line * 8 + col - 24] = 1
                        else:
                            (first if quarter < 2 else second)[row, line * 24 + col] = 1
    return first, second, halo


def place_stacked():
    body = np.zeros((576, 288), np.float32)
    last = np.zeros((576, 144), np.float32)
    tail = np.zeros((576, 144), np.float32)
    for a in range(2):
        for b in range(2):
            for pair in range(2):
                for level in range(2):
                    for i in range(12):
                        for j in range(3):
                            row = (a * 2 + b) * 144 + pair * 72 + level * 36 + i * 3 + j
                            quarter, lon, lat = i // 3, 2 * (i % 3) + a, 2 * j + b
                            inner = level * 36 + lat * 6 + lon
                            if quarter == 0:
                                tail[row, pair * 72 + inner] = 1
                            elif quarter == 3:
                                last[row, pair * 72 + inner] = 1
                            else:
                                body[row, pair * 144 + (quarter - 1) * 72 + inner] = 1
    return body, last, tail


def place_result():
    body = np.zeros((576, 288), np.float32)
    last = np.zeros((576, 144), np.float32)
    tail = np.zeros((576, 144), np.float32)
    for level in range(4):
        for lat in range(6):
            for lon in range(24):
                row = (level * 6 + lat) * 24 + lon
                inner = (level % 2) * 36 + lat * 6 + lon % 6
                if lon < 6:
                    tail[row, (level // 2) * 72 + inner] = 1
                elif lon >= 18:
                    last[row, (level // 2) * 72 + inner] = 1
                else:
                    body[row, (level // 2) * 144 + (lon // 6 - 1) * 72 + inner] = 1
    return body, last, tail


def dot(a, b):
    return lax.dot_general(a, b, (((1,), (0,)), ((), ())), preferred_element_type=F32)


def dot_nt(a, b):
    return lax.dot_general(a, b, (((1,), (1,)), ((), ())), preferred_element_type=F32)


def dot_tn(a, b):
    return lax.dot_general(a, b, (((0,), (0,)), ((), ())), preferred_element_type=F32)


def steps(count, body):
    lax.fori_loop(0, count, lambda i, carry: (body(i), carry)[1], 0)


def span(i, size):
    return pl.ds(pl.multiple_of(i * size, size), size)


def total(x):
    return jnp.sum(x, axis=-1, keepdims=True)


def norm_parts(parts):
    width = sum(p.shape[1] for p in parts)
    mean = sum(total(p) for p in parts) * (1.0 / width)
    centred = [p - mean for p in parts]
    rstd = lax.rsqrt(sum(total(c * c) for c in centred) * (1.0 / width) + NORM_EPS)
    return [c * rstd for c in centred], rstd


def norm_back(normed, rstd, upstream):
    width = sum(p.shape[1] for p in normed)
    first = sum(total(u) for u in upstream) * (1.0 / width)
    second = sum(total(u * n) for u, n in zip(upstream, normed)) * (1.0 / width)
    return [rstd * (u - first - n * second) for u, n in zip(upstream, normed)]


def half_masks(rows):
    lane = lax.broadcasted_iota(jnp.int32, (rows, 128), 1)
    low = lane < 64
    return low, jnp.where(low, 1.0, 0.0).astype(BF), jnp.where(low, 0.0, 1.0).astype(BF)


def two_heads(x, masks):
    return jnp.concatenate([x * masks[1], x * masks[2]], axis=0)


def one_row(x, masks):
    rows = x.shape[0] // 2
    return jnp.where(masks[0], x[:rows], x[rows:])


def softmax(scores):
    shifted = jnp.exp(scores - jnp.max(scores, axis=0, keepdims=True))
    return shifted * (1.0 / jnp.sum(shifted, axis=0, keepdims=True))


def attend_back(queries, keys, values, d_context, probs, weights, masks):
    d_weights = dot_nt(values, d_context)
    mean = jnp.sum(d_weights * probs, axis=0, keepdims=True)
    d_scores = (probs * (d_weights - mean)).astype(BF)
    d_queries = one_row(dot_tn(d_scores, keys), masks)
    return d_queries, dot(d_scores, queries), dot(weights, d_context)


def axis_places():
    lon, lat = lax.axis_index("lon"), lax.axis_index("lat")
    return jnp.stack([lon >> 2, (lon >> 1) & 1, lon & 1, lat >> 1, lat & 1]).astype(jnp.int32)


def row_choice(place, rows, features, per_share, both_halves):
    r = lax.broadcasted_iota(jnp.int32, (rows, features), 0)
    col = lax.broadcasted_iota(jnp.int32, (rows, features), 1)
    low = r & (per_share - 1)
    r = r >> (per_share.bit_length() - 1)
    if both_halves:
        x_hi = (r & 1) ^ place[4]
        r = r >> 1
    else:
        x_hi = place[4]
    x_lo = (r & 1) ^ place[1]
    z = ((r >> 1) + place[3]) & 3
    core = ((r >> 3) & 1) ^ place[2]
    share = ((x_lo * 2 + core) * 8) + z * 2 + x_hi
    return jnp.where(share * per_share + low == col, 1.0, 0.0).astype(BF)


def interleave(own, far):
    return jnp.concatenate([own[:72], far[:72], own[72:], far[72:]], axis=0)


def first_rows(x):
    return jnp.concatenate([x[0:72], x[144:216]], axis=0)


def last_rows(x):
    return jnp.concatenate([x[72:144], x[216:288]], axis=0)


def fetch(sems, *pairs):
    copies = [pltpu.make_async_copy(src, dst, sems.at[i]) for i, (src, dst) in enumerate(pairs)]
    for copy in copies:
        copy.start()
    return copies


def fine_forward_kernel(*refs, with_halo):
    if with_halo:
        tok, halo, put, put_halo, w_qkv_in, w_out_in, last, tail = refs[:8]
    else:
        tok, put, w_qkv_in, w_out_in, result_out = refs[:5]
    x_out, qkv_out, ctx_out, prob_out, w_qkv, w_out, sems = refs[-7:]
    loads = fetch(sems, (w_qkv_in, w_qkv), (w_out_in, w_out))
    x = dot(put[...], tok[...])
    if with_halo:
        x = x + dot(put_halo[...], halo[...])
    x_out[...] = x.astype(BF)
    (normed,), _ = norm_parts([x])
    normed = normed.astype(BF)
    loads[0].wait()
    for n in range(3):
        part = dot(normed, w_qkv[:, n * 512 : (n + 1) * 512])
        if n == 0:
            part = part * (512 // HEADS) ** (-0.5)
        qkv_out[:, n * 512 : (n + 1) * 512] = part.astype(BF)
    masks = half_masks(144)
    for w in range(2):
        rows = slice(w * 144, (w + 1) * 144)
        for h in range(4):
            lanes = slice(h * 128, (h + 1) * 128)
            queries = two_heads(qkv_out[rows, lanes], masks)
            keys = qkv_out[rows, 512 + h * 128 : 512 + (h + 1) * 128]
            values = qkv_out[rows, 1024 + h * 128 : 1024 + (h + 1) * 128]
            weights = softmax(dot_nt(keys, queries)).astype(BF)
            prob_out[w * 4 + h] = weights
            ctx_out[rows, lanes] = one_row(dot_tn(weights, values), masks).astype(BF)
    loads[1].wait()
    result = x + dot(ctx_out[...], w_out[...])
    if with_halo:
        last[...] = first_rows(result).astype(BF)
        tail[...] = last_rows(result).astype(BF)
    else:
        result_out[...] = result.astype(BF)


def cotangent_kernel(cot_own, cot_far, w_out, cot, d_ctx):
    cot[...] = interleave(cot_own[...].astype(F32), cot_far[...].astype(F32)).astype(BF)
    for n in range(2):
        lanes = slice(n * 512, (n + 1) * 512)
        d_ctx[:, lanes] = dot_nt(cot[...], w_out[lanes, :]).astype(BF)


def coarse_kernel(
    place_ref,
    body_own,
    last_own,
    tail_own,
    body_far,
    last_far,
    tail_far,
    put_body,
    put_last,
    put_tail,
    cot,
    d_ctx,
    w_merge_in,
    w_qkv_in,
    merged_ref,
    ctx_ref,
    d_qkv_ref,
    stacked_out,
    send,
    keep,
    normed_ref,
    qkv_ref,
    left_qkv,
    left_out,
    w_merge,
    w_qkv,
    sems,
    factor,
):
    loads = fetch(sems, (w_merge_in, w_merge), (w_qkv_in, w_qkv))
    place = [place_ref[i] for i in range(5)]

    def stack(body, last, tail):
        return (
            dot(put_body[...], body[...])
            + dot(put_last[...], last[...])
            + dot(put_tail[...], tail[...])
        )

    own = stack(body_own, last_own, tail_own)
    far = stack(body_far, last_far, tail_far)
    parts = [interleave(own[g * 144 : (g + 1) * 144], far[g * 144 : (g + 1) * 144]) for g in range(4)]
    for g in range(4):
        stacked_out[g] = parts[g].astype(BF)
    normed, _ = norm_parts(parts)
    loads[0].wait()
    merged = sum(dot(normed[g].astype(BF), w_merge[g * 512 : (g + 1) * 512, :]) for g in range(4))
    merged_ref[...] = merged.astype(BF)
    merged = merged_ref[...].astype(F32)
    (normed,), _ = norm_parts([merged])
    normed_ref[...] = normed.astype(BF)
    loads[1].wait()

    def project(n):
        part = dot(normed_ref[...], w_qkv[:, span(n, 512)])
        scale = jnp.where(n < 2, (1024 // HEADS2) ** (-0.5), 1.0)
        qkv_ref[:, span(n, 512)] = (part * scale).astype(BF)

    steps(6, project)
    masks = half_masks(144)
    for h in range(8):
        lanes, key_lanes, value_lanes = (slice(n * 128, (n + 1) * 128) for n in (h, h + 8, h + 16))
        for pair in range(2):
            rows = slice(pair * 144, (pair + 1) * 144)
            queries = two_heads(qkv_ref[rows, lanes], masks)
            keys = qkv_ref[rows, key_lanes]
            values = qkv_ref[rows, value_lanes]
            d_context = two_heads(d_ctx[rows, lanes], masks)
            probs = softmax(dot_nt(keys, queries))
            weights = probs.astype(BF)
            ctx_ref[rows, lanes] = one_row(dot_tn(weights, values), masks).astype(BF)
            d_queries, d_keys, d_values = attend_back(
                queries, keys, values, d_context, probs, weights, masks
            )
            d_qkv_ref[rows, lanes] = (d_queries * (1024 // HEADS2) ** (-0.5)).astype(BF)
            d_qkv_ref[rows, key_lanes] = d_keys.astype(BF)
            d_qkv_ref[rows, value_lanes] = d_values.astype(BF)

    choice = row_choice(place, 128, 256, 8, False)
    for y in range(4):
        lanes = span((place[0] + y) & 3, 256)
        block = dot_nt(choice, normed_ref[:, lanes]).astype(BF)
        other = dot_nt(choice, ctx_ref[:, lanes]).astype(BF)
        for cz in range(8):
            rows = slice((cz * 4 + y) * 16, (cz * 4 + y + 1) * 16)
            left_qkv[rows] = block[cz * 16 : (cz + 1) * 16]
            left_out[rows] = other[cz * 16 : (cz + 1) * 16]

    def grads_qkv(n):
        part = (dot(left_qkv[...], d_qkv_ref[:, span(n, 512)]) * factor).astype(BF)
        keep[:, span(n, 512)] = part[:256]
        send[:, span(n, 512)] = part[256:]

    steps(6, grads_qkv)

    def grads_out(n):
        part = (dot(left_out[...], cot[:, span(n, 512)]) * factor).astype(BF)
        keep[:, span(n + 6, 512)] = part[:256]
        send[:, span(n + 6, 512)] = part[256:]

    steps(2, grads_out)


def merge_back_kernel(
    place_ref,
    merged,
    ctx,
    d_qkv,
    stacked,
    cot,
    put_body,
    put_last,
    put_tail,
    w_qkv_in,
    w_merge_in,
    w_out_in,
    coarse,
    d_body,
    d_last,
    d_tail,
    send,
    keep,
    normed_ref,
    d_merged_ref,
    d_stacked_ref,
    left,
    w_qkv,
    w_merge,
    w_out,
    sems,
    factor,
):
    loads = fetch(sems, (w_qkv_in, w_qkv), (w_merge_in, w_merge), (w_out_in, w_out))
    place = [place_ref[i] for i in range(5)]
    stack_normed, stack_rstd = norm_parts([stacked[g].astype(F32) for g in range(4)])
    for g in range(4):
        normed_ref[g] = stack_normed[g].astype(BF)
    loads[0].wait()
    d_normed = jnp.zeros((288, 1024), F32)
    for n in range(3):
        d_normed = d_normed + dot_nt(
            d_qkv[:, n * 1024 : (n + 1) * 1024], w_qkv[:, n * 1024 : (n + 1) * 1024]
        )
    d_normed = d_normed.astype(BF).astype(F32)
    (normed,), rstd = norm_parts([merged[...].astype(F32)])
    (d_input,) = norm_back([normed], rstd, [d_normed])
    d_input = cot[...].astype(F32) + d_input
    d_merged_ref[...] = d_input.astype(BF)
    d_own = first_rows(d_input).astype(BF)

    loads[1].wait()
    upstream = []
    for g in range(4):
        part = dot_nt(d_own, w_merge[g * 512 : (g + 1) * 512, :])
        upstream.append(part.astype(BF).astype(F32))
    own = norm_back([first_rows(n) for n in stack_normed], first_rows(stack_rstd), upstream)
    for g in range(4):
        d_stacked_ref[g * 144 : (g + 1) * 144, :] = own[g].astype(BF)
    d_tail[...] = dot(put_tail[...], d_stacked_ref[...]).astype(BF)
    d_body[...] = dot(put_body[...], d_stacked_ref[...]).astype(BF)
    d_last[...] = dot(put_last[...], d_stacked_ref[...]).astype(BF)

    choice = row_choice(place, 256, 512, 16, False)
    for y in range(4):
        block = dot_nt(choice, normed_ref[(place[0] + y) & 3])
        for cz in range(8):
            for half in range(2):
                start = cz * 32 + half * 8
                rows = jnp.concatenate([block[start : start + 8], block[start + 16 : start + 24]], axis=0)
                left[half, (cz * 4 + y) * 16 : (cz * 4 + y + 1) * 16] = rows.astype(BF)
    for n in range(4):
        columns = slice(n * 512, (n + 1) * 512)
        part = dot(left[n // 2], d_merged_ref[:, (n % 2) * 512 : (n % 2 + 1) * 512])
        part = (part * factor).astype(BF)
        keep[:, columns] = part[:256]
        send[:, columns] = part[256:]

    loads[2].wait()
    projected = dot(ctx[...], w_out[...])
    coarse[...] = first_rows(merged[...].astype(F32) + projected).astype(BF)


def windows_back(d_res, qkv, prob, d_ctx_ref, d_qkv_ref, w_out, first):
    d_ctx_ref[...] = dot_nt(d_res[...], w_out[...]).astype(BF)
    masks = half_masks(144)
    for w in range(2):
        rows = slice(w * 144, (w + 1) * 144)
        put = slice(first + w * 144, first + (w + 1) * 144)
        for h in range(4):
            lanes = slice(h * 128, (h + 1) * 128)
            key_lanes = slice(512 + h * 128, 512 + (h + 1) * 128)
            value_lanes = slice(1024 + h * 128, 1024 + (h + 1) * 128)
            weights = prob[w * 4 + h]
            d_queries, d_keys, d_values = attend_back(
                two_heads(qkv[rows, lanes], masks),
                qkv[rows, key_lanes],
                qkv[rows, value_lanes],
                two_heads(d_ctx_ref[rows, lanes], masks),
                weights.astype(F32),
                weights,
                masks,
            )
            d_qkv_ref[put, lanes] = (d_queries * (512 // HEADS) ** (-0.5)).astype(BF)
            d_qkv_ref[put, key_lanes] = d_keys.astype(BF)
            d_qkv_ref[put, value_lanes] = d_values.astype(BF)


def input_back(d_res, d_qkv, x, w_qkv):
    (normed,), rstd = norm_parts([x[...].astype(F32)])
    d_normed = dot_nt(d_qkv[...], w_qkv[...]).astype(BF).astype(F32)
    (d_input,) = norm_back([normed], rstd, [d_normed])
    return d_res[...].astype(F32) + d_input


def first_back_kernel(
    d_res, x, qkv, prob_in, w_qkv_in, w_out_in, d_qkv, d_x, d_ctx_ref, prob, w_qkv, w_out, sems
):
    loads = fetch(sems, (w_out_in, w_out), (prob_in, prob), (w_qkv_in, w_qkv))
    loads[0].wait()
    loads[1].wait()
    windows_back(d_res, qkv, prob, d_ctx_ref, d_qkv, w_out, 0)
    loads[2].wait()
    d_x[...] = input_back(d_res, d_qkv, x, w_qkv).astype(BF)


def second_back_kernel(
    place_ref,
    d_last,
    d_tail,
    d_first,
    d_qkv_first,
    x_first,
    x_second,
    ctx_first,
    ctx_second,
    qkv,
    prob,
    w_out,
    d_res_out,
    d_qkv_out,
    send,
    keep,
    normed_ref,
    ctx_ref,
    d_ctx_ref,
    d_res_ref,
    d_qkv_ref,
    left_qkv,
    left_out,
    factor,
):
    place = [place_ref[i] for i in range(5)]
    d_res_out[...] = interleave(d_last[...].astype(F32), d_tail[...].astype(F32)).astype(BF)
    windows_back(d_res_out, qkv, prob, d_ctx_ref, d_qkv_ref, w_out, 288)
    d_qkv_out[...] = d_qkv_ref[288:576]
    for half, (x, ctx, d_res) in enumerate(
        ((x_first, ctx_first, d_first), (x_second, ctx_second, d_res_out))
    ):
        rows = slice(half * 288, (half + 1) * 288)
        (normed,), _ = norm_parts([x[...].astype(F32)])
        normed_ref[rows] = normed.astype(BF)
        ctx_ref[rows] = ctx[...]
        d_res_ref[rows] = d_res[...]
    d_qkv_ref[0:288] = d_qkv_first[...]
    choice = row_choice(place, 128, 128, 4, True)
    for y in range(4):
        lanes = span((place[0] + y) & 3, 128)
        block = dot_nt(choice, normed_ref[:, lanes]).astype(BF)
        other = dot_nt(choice, ctx_ref[:, lanes]).astype(BF)
        for cz in range(8):
            rows = slice((cz * 4 + y) * 16, (cz * 4 + y + 1) * 16)
            left_qkv[rows] = block[cz * 16 : (cz + 1) * 16]
            left_out[rows] = other[cz * 16 : (cz + 1) * 16]
    for n in range(4):
        columns = slice(n * 512, (n + 1) * 512)
        if n < 3:
            part = dot(left_qkv[...], d_qkv_ref[:, columns])
        else:
            part = dot(left_out[...], d_res_ref[...])
        part = (part * factor).astype(BF)
        keep[:, columns] = part[:256]
        send[:, columns] = part[256:]


def last_back_kernel(d_res, d_qkv, x, w_qkv, d_last, d_tail):
    d_input = input_back(d_res, d_qkv, x, w_qkv)
    d_last[...] = first_rows(d_input).astype(BF)
    d_tail[...] = last_rows(d_input).astype(BF)


def place_result_kernel(body, last, tail, put_body, put_last, put_tail, out):
    out[...] = (
        dot(put_body[...], body[...]) + dot(put_last[...], last[...]) + dot(put_tail[...], tail[...])
    ).astype(BF)


def call(kernel, outs, scratch=(), scalars=0, far=(), us=1, room=4, after=(), limit=None, through=()):
    def run(*args):
        in_specs = [
            pl.BlockSpec(memory_space=pltpu.SMEM if i < scalars else pl.ANY if i in far else pltpu.VMEM)
            for i in range(len(args))
        ]
        held = sum(a.size * a.dtype.itemsize for i, a in enumerate(args) if i not in far)
        held += sum(int(np.prod(s)) * jnp.dtype(d).itemsize for s, d in outs)
        held += sum(int(np.prod(s)) * jnp.dtype(d).itemsize for s, d in scratch)
        shapes = [pltpu.VMEM(shape, dtype) for shape, dtype in scratch]
        if far:
            shapes.append(pltpu.SemaphoreType.DMA((len(far),)))
        body = kernel
        idle = len(through) + len(after)
        if idle:

            def body(*refs):
                refs = refs[: len(args)] + refs[len(args) + idle :]
                results = len(args) + len(outs)
                kernel(*refs[:results], *refs[results + len(through) :])

        return pl.pallas_call(
            body,
            out_shape=[jax.ShapeDtypeStruct(shape, dtype) for shape, dtype in outs]
            + [jax.ShapeDtypeStruct(a.shape, a.dtype) for a in through],
            in_specs=in_specs + [pl.BlockSpec(memory_space=pl.ANY)] * idle,
            out_specs=[VMEM] * len(outs) + [pl.BlockSpec(memory_space=pl.ANY)] * len(through),
            input_output_aliases={len(args) + i: len(outs) + i for i in range(len(through))},
            scratch_shapes=shapes,
            cost_estimate=pl.CostEstimate(
                flops=int(us * 1e9), bytes_accessed=int(us * 3e6), transcendentals=0
            ),
            compiler_params=pltpu.CompilerParams(
                vmem_limit_bytes=limit * MIB if limit else int(held * 1.15) + room * MIB
            ),
        )(*args, *through, *after)

    return run


def route(move):
    pairs = []
    for source in range(128):
        lon, lat = divmod(source, 8)
        y, x_lo, core, z, x_hi = move(lon >> 2, (lon >> 1) & 1, lon & 1, lat >> 1, lat & 1)
        pairs.append((source, (((y & 3) * 2 + x_lo) * 2 + core) * 8 + (z & 3) * 2 + x_hi))
    return pairs


def send_core(x):
    return lax.ppermute(x, ("lon", "lat"), route(lambda y, xl, c, z, xh: (y, xl, 1 - c, z, xh)))


def send_z(x, d):
    return lax.ppermute(x, ("lon", "lat"), route(lambda y, xl, c, z, xh: (y, xl, c, z + d, xh)))


def send_y(x, d):
    return lax.ppermute(x, ("lon", "lat"), route(lambda y, xl, c, z, xh: (y + d, xl, c, z, xh)))


def send_x_lo(x):
    return lax.ppermute(x, ("lon", "lat"), route(lambda y, xl, c, z, xh: (y, 1 - xl, c, z, xh)))


def send_x_hi(x):
    return lax.ppermute(x, ("lon", "lat"), route(lambda y, xl, c, z, xh: (y, xl, c, z, 1 - xh)))


def send_lon(x, step, partner):
    pairs = []
    for lon in range(16):
        for lat in range(8):
            pairs.append((lon * 8 + lat, (lon + step) % 16 * 8 + (lat ^ partner)))
    return lax.ppermute(x, ("lon", "lat"), pairs)


def send_x_both(x):
    return lax.ppermute(x, ("lon", "lat"), route(lambda y, xl, c, z, xh: (y, 1 - xl, c, z, 1 - xh)))


def add(*refs):
    return sum(r.astype(F32) for r in refs)


def wide_split_kernel(keep_a, got_a, keep_m, got_m, *pieces):
    def by_z(d, o):
        return (
            add(keep_a[d, o, :, :2048], got_a[d, o, :, :2048]).astype(BF),
            add(keep_m[d, o, :, :1024], got_m[d, o, :, :1024]).astype(BF),
        )

    def by_y(d, o):
        return (
            add(keep_a[o, d, :, 2048:], got_a[o, d, :, 2048:]).astype(BF),
            add(keep_m[o, d, :, 1024:], got_m[o, d, :, 1024:]).astype(BF),
        )

    for ring, block in ((pieces[:5], by_z), (pieces[5:], by_y)):
        for d, ref in ((0, ring[0]), (1, ring[1]), (3, ring[2])):
            for o in range(4):
                ref[o, :, :2048], ref[o, :, 2048:] = block(d, o)
        for o in range(4):
            ref = ring[3 + o // 2]
            ref[o % 2, :, :2048], ref[o % 2, :, 2048:] = block(2, o)


def wide_pass_kernel(*refs):
    for ring in range(2):
        up, down, from_below, from_above, up_out, down_out = refs[ring * 4 : ring * 4 + 4] + refs[8 + ring * 2 : 10 + ring * 2]
        for o in range(4):
            if o < 2:
                up_out[o] = add(up[o], from_below[o]).astype(BF)
                down_out[o] = down[o]
            else:
                up_out[o] = up[o]
                down_out[o] = add(down[o], from_above[o - 2]).astype(BF)


def wide_sum_kernel(*refs):
    for ring in range(2):
        parts, out = refs[ring * 3 : ring * 3 + 3], refs[6 + ring]
        for d in range(4):
            out[d] = add(*(r[d] for r in parts)).astype(BF)


def joint_split_kernel(first, last, keep, got, *refs):
    to_y, to_z = refs[:4], refs[4:]
    for d in range(4):
        to_y[d][:, :3072] = first[d]
        to_z[d][:, :3072] = last[d]
        for o in range(4):
            columns = slice(3072 + o * 1024, 3072 + (o + 1) * 1024)
            to_y[d][:, columns] = add(keep[o, d, :, 1024:], got[o, d, :, 1024:]).astype(BF)
            to_z[d][:, columns] = add(keep[d, o, :, :1024], got[d, o, :, :1024]).astype(BF)


def joint_sum_kernel(*refs):
    from_y, from_z, wide_keep, wide_send, to_y, to_z = (
        refs[:4],
        refs[4:8],
        refs[8],
        refs[9],
        refs[10:14],
        refs[14:18],
    )
    first = add(*(r[:, :3072] for r in from_y)).astype(BF).astype(F32)
    last = add(*(r[:, :3072] for r in from_z)).astype(BF).astype(F32)
    for wide, rows in ((wide_keep, slice(0, 8)), (wide_send, slice(8, 16))):
        wide[:, :3072] = first[rows].astype(BF)
        wide[:, 3072:] = last[rows].astype(BF)
    for d in range(4):
        columns = slice(3072 + d * 1024, 3072 + (d + 1) * 1024)
        to_y[d][...] = add(*(r[:, columns] for r in from_z)).astype(BF)
        to_z[d][...] = add(*(r[:, columns] for r in from_y)).astype(BF)


def fine_split_kernel(*refs):
    first, last = add(*(r[...] for r in refs[:4])), add(*(r[...] for r in refs[4:8]))
    for place in range(4):
        refs[8 + place][:, :1024] = first[place * 4 : (place + 1) * 4].astype(BF)
        refs[8 + place][:, 1024:] = last[place * 4 : (place + 1) * 4].astype(BF)


def shares_kernel(own, lo, hi, both, wide_keep, wide_got, fine_qkv, fine_out, merge, coarse_qkv, coarse_out):
    fine = add(own[...], lo[...], hi[...], both[...])
    fine_qkv[...] = fine[:, :1536]
    fine_out[...] = fine[:, 1536:]
    wide = add(wide_keep[...], wide_got[...])
    coarse_qkv[:, :2048] = wide[:, :2048]
    coarse_qkv[:, 2048:] = wide[:, 3072:4096]
    coarse_out[...] = wide[:, 4096:5120]
    merge[0:8] = wide[:, 2048:3072]
    merge[8:16] = wide[:, 5120:6144]


def spread_z(pieces):
    return [pieces[0]] + [send_z(pieces[d], d) for d in (1, 3, 2)]


def spread_y(pieces):
    return [pieces[0]] + [send_y(pieces[d], d) for d in (1, 3, 2)]


def blocks(x):
    return x.reshape(4, 4, 16, x.shape[1])


def local(tokens, cotangent, fine_qkv, fine_out, merge_weight, coarse_qkv, coarse_out):
    factor = (144 * lax.axis_size("lon") * lax.axis_size("lat")) ** (-0.5)
    place = axis_places()
    put_first, put_second, put_halo = (jnp.asarray(a, BF) for a in place_tokens())
    stack = place_stacked()
    unstack = [jnp.asarray(a.T, BF) for a in stack]
    stack = [jnp.asarray(a, BF) for a in stack]
    result = [jnp.asarray(a, BF) for a in place_result()]

    tok = tokens.transpose(0, 2, 1, 3)
    halo = send_lon(tok[:, :, :8], -1, 0).reshape(192, 512)
    tok = tok.reshape(576, 512)

    stash = [((288, 512), BF), ((288, 1536), BF), ((288, 512), BF), ((8, 144, 288), BF)]
    fine_weights = [((512, 1536), BF), ((512, 512), BF)]
    body, x_first, qkv_first, ctx_first, prob_first = call(
        functools.partial(fine_forward_kernel, with_halo=False),
        [((288, 512), BF)] + stash,
        fine_weights,
        far=(2, 3),
        us=6,
        limit=60,
    )(tok, put_first, fine_qkv, fine_out)
    body_far = send_lon(body, 0, 1)
    cotangent, body = lax.optimization_barrier((cotangent, body))
    cot_own = cotangent.reshape(144, 1024)
    cot_far = send_lon(cot_own, 0, 1)
    last, tail, x_second, qkv_second, ctx_second, prob_second = call(
        functools.partial(fine_forward_kernel, with_halo=True),
        [((144, 512), BF)] * 2 + stash,
        fine_weights,
        far=(4, 5),
        us=6,
        limit=60,
    )(tok, halo, put_second, put_halo, fine_qkv, fine_out)
    tail_own = send_lon(tail, 1, 0)
    tail_far = send_lon(tail, 1, 1)
    last_far = send_lon(last, 0, 1)
    cot, d_ctx = call(cotangent_kernel, [((288, 1024), BF)] * 2, us=3)(cot_own, cot_far, coarse_out)

    merged, ctx, d_qkv, stacked, send_a, keep_a = call(
        functools.partial(coarse_kernel, factor=factor),
        [
            ((288, 1024), BF),
            ((288, 1024), BF),
            ((288, 3072), BF),
            ((4, 288, 512), BF),
            ((256, 4096), BF),
            ((256, 4096), BF),
        ],
        [
            ((288, 1024), BF),
            ((288, 3072), BF),
            ((512, 288), BF),
            ((512, 288), BF),
            ((2048, 1024), BF),
            ((1024, 3072), BF),
        ],
        scalars=1,
        far=(12, 13),
        us=20,
        room=8,
    )(
        place,
        body,
        last,
        tail_own,
        body_far,
        last_far,
        tail_far,
        *stack,
        cot,
        d_ctx,
        merge_weight,
        coarse_qkv,
    )
    got_a = send_core(send_a)

    coarse, d_first, d_last, d_tail, send_m, keep_m = call(
        functools.partial(merge_back_kernel, factor=factor),
        [
            ((144, 1024), BF),
            ((288, 512), BF),
            ((144, 512), BF),
            ((144, 512), BF),
            ((256, 2048), BF),
            ((256, 2048), BF),
        ],
        [
            ((4, 288, 512), BF),
            ((288, 1024), BF),
            ((576, 512), BF),
            ((2, 512, 288), BF),
            ((1024, 3072), BF),
            ((2048, 1024), BF),
            ((1024, 1024), BF),
        ],
        scalars=1,
        far=(9, 10, 11),
        us=12,
        room=8,
    )(place, merged, ctx, d_qkv, stacked, cot, *unstack, coarse_qkv, merge_weight, coarse_out)
    d_tail = send_lon(d_tail, -1, 0)
    got_m = send_core(send_m)

    ring_shapes = ([((4, 16, 3072), BF)] * 3 + [((2, 16, 3072), BF)] * 2) * 2
    pieces = call(wide_split_kernel, ring_shapes, us=4)(
        blocks(keep_a), blocks(got_a), blocks(keep_m), blocks(got_m)
    )
    wide_z, wide_y = pieces[:5], pieces[5:]
    passed = (
        send_z(wide_z[3], 1),
        send_z(wide_z[4], -1),
        send_y(wide_y[3], 1),
        send_y(wide_y[4], -1),
    )

    d_qkv_first, d_x_first = call(
        first_back_kernel,
        [((288, 1536), BF), ((288, 512), BF)],
        [((288, 512), BF), ((8, 144, 288), BF)] + fine_weights,
        far=(3, 4, 5),
        us=8,
        after=(pieces[0],),
    )(d_first, x_first, qkv_first, prob_first, fine_qkv, fine_out)

    up_z, down_z, up_y, down_y = call(
        wide_pass_kernel, [((4, 16, 3072), BF)] * 4, us=2, after=(d_qkv_first,)
    )(wide_z[1], wide_z[2], *passed[:2], wide_y[1], wide_y[2], *passed[2:])
    wide_z = (wide_z[0], send_z(up_z, 1), send_z(down_z, -1))
    wide_y = (wide_y[0], send_y(up_y, 1), send_y(down_y, -1))

    d_res, d_qkv_second, send_f, keep_f = call(
        functools.partial(second_back_kernel, factor=factor),
        [((288, 512), BF), ((288, 1536), BF), ((256, 2048), BF), ((256, 2048), BF)],
        [
            ((576, 512), BF),
            ((576, 512), BF),
            ((288, 512), BF),
            ((576, 512), BF),
            ((576, 1536), BF),
            ((512, 576), BF),
            ((512, 576), BF),
        ],
        scalars=1,
        us=10,
        after=(up_z,),
    )(
        place,
        d_last,
        d_tail,
        d_first,
        d_qkv_first,
        x_first,
        x_second,
        ctx_first,
        ctx_second,
        qkv_second,
        prob_second,
        fine_out,
    )
    wide_first, wide_last, send_f = call(
        wide_sum_kernel, [((4, 16, 3072), BF)] * 2, us=2, through=(send_f,)
    )(*wide_z, *wide_y)
    got_f = send_core(send_f)
    d_x_last, d_x_tail = call(last_back_kernel, [((144, 512), BF)] * 2, us=0.01)(
        d_res, d_qkv_second, x_second, fine_qkv
    )
    d_x_tail = send_lon(d_x_tail, 1, 0)

    pieces = call(joint_split_kernel, [((16, 7168), BF)] * 8, us=3, after=(d_x_last,))(
        wide_first, wide_last, blocks(keep_f), blocks(got_f)
    )
    from_y, from_z = spread_y(pieces[:4]), spread_z(pieces[4:])
    (d_tokens,) = call(place_result_kernel, [((576, 512), BF)], us=2)(
        d_x_first, d_x_last, d_x_tail, *result
    )
    pieces = call(
        joint_sum_kernel,
        [((8, 6144), BF)] * 2 + [((16, 1024), BF)] * 8,
        us=2,
    )(*from_y, *from_z)
    wide_keep, wide_send = pieces[:2]
    wide_got = send_x_lo(wide_send)
    from_y, from_z = spread_y(pieces[2:6]), spread_z(pieces[6:])
    own, hi, lo, both = call(fine_split_kernel, [((4, 2048), BF)] * 4, after=(d_tokens,))(*from_y, *from_z)
    lo, hi, both = send_x_lo(lo), send_x_hi(hi), send_x_both(both)
    shares = call(
        shares_kernel,
        [
            ((4, 1536), F32),
            ((4, 512), F32),
            ((16, 1024), F32),
            ((8, 3072), F32),
            ((8, 1024), F32),
        ],
    )(own, lo, hi, both, wide_keep, wide_got)
    return (
        coarse.reshape(4, 12, 3, 1024),
        d_tokens.reshape(4, 6, 24, 512).transpose(0, 2, 1, 3),
        *shares,
    )


def solution(mesh):
    grid_spec = P(None, "lon", "lat", None)
    rows_spec = P(("lon", "lat"), None)
    return jax.shard_map(
        local,
        mesh=mesh,
        in_specs=(grid_spec, grid_spec, P(), P(), P(), P(), P()),
        out_specs=(grid_spec, grid_spec) + (rows_spec,) * 5,
        check_vma=False,
    )
```

```python
import functools

import jax
import jax.numpy as jnp
import numpy as np
from jax import lax
from jax.experimental import pallas as pl
from jax.experimental.pallas import tpu as pltpu
from jax.sharding import PartitionSpec as P

HEADS = 8
HEADS2 = 16
NORM_EPS = 1e-05
BF = jnp.bfloat16
F32 = jnp.float32
VMEM = pl.BlockSpec(memory_space=pltpu.VMEM)
MIB = 1024 * 1024


def place_tokens():
    own = np.zeros((432, 576), np.float32)
    halo = np.zeros((144, 192), np.float32)
    for pair in range(2):
        for quarter in range(4):
            for level in range(2):
                for lat in range(6):
                    for lon in range(6):
                        inner = level * 36 + lat * 6 + lon
                        line = (2 * pair + level) * 6 + lat
                        if quarter < 2:
                            own[pair * 144 + quarter * 72 + inner, line * 24 + 6 * quarter + lon + 6] = 1
                        elif quarter == 2:
                            own[288 + pair * 72 + inner, line * 24 + lon + 18] = 1
                        else:
                            halo[pair * 72 + inner, line * 8 + lon] = 1
    return own, halo


def place_stacked():
    body = np.zeros((576, 288), np.float32)
    last = np.zeros((576, 144), np.float32)
    tail = np.zeros((576, 144), np.float32)
    for a in range(2):
        for b in range(2):
            for pair in range(2):
                for level in range(2):
                    for i in range(12):
                        for j in range(3):
                            row = (a * 2 + b) * 144 + pair * 72 + level * 36 + i * 3 + j
                            quarter, lon, lat = i // 3, 2 * (i % 3) + a, 2 * j + b
                            inner = level * 36 + lat * 6 + lon
                            if quarter == 0:
                                tail[row, pair * 72 + inner] = 1
                            elif quarter == 3:
                                last[row, pair * 72 + inner] = 1
                            else:
                                body[row, pair * 144 + (quarter - 1) * 72 + inner] = 1
    return body, last, tail


def place_result():
    body = np.zeros((576, 288), np.float32)
    last = np.zeros((576, 144), np.float32)
    tail = np.zeros((576, 144), np.float32)
    for level in range(4):
        for lat in range(6):
            for lon in range(24):
                row = (level * 6 + lat) * 24 + lon
                inner = (level % 2) * 36 + lat * 6 + lon % 6
                if lon < 6:
                    tail[row, (level // 2) * 72 + inner] = 1
                elif lon >= 18:
                    last[row, (level // 2) * 72 + inner] = 1
                else:
                    body[row, (level // 2) * 144 + (lon // 6 - 1) * 72 + inner] = 1
    return body, last, tail


def dot(a, b):
    return lax.dot_general(a, b, (((1,), (0,)), ((), ())), preferred_element_type=F32)


def dot_nt(a, b):
    return lax.dot_general(a, b, (((1,), (1,)), ((), ())), preferred_element_type=F32)


def dot_tn(a, b):
    return lax.dot_general(a, b, (((0,), (0,)), ((), ())), preferred_element_type=F32)


def steps(count, body):
    lax.fori_loop(0, count, lambda i, carry: (body(i), carry)[1], 0)


def span(i, size):
    return pl.ds(pl.multiple_of(i * size, size), size)


def total(x):
    return jnp.sum(x, axis=-1, keepdims=True)


def norm_parts(parts):
    width = sum(p.shape[1] for p in parts)
    mean = sum(total(p) for p in parts) * (1.0 / width)
    centred = [p - mean for p in parts]
    rstd = lax.rsqrt(sum(total(c * c) for c in centred) * (1.0 / width) + NORM_EPS)
    return [c * rstd for c in centred], rstd


def norm_back(normed, rstd, upstream):
    width = sum(p.shape[1] for p in normed)
    first = sum(total(u) for u in upstream) * (1.0 / width)
    second = sum(total(u * n) for u, n in zip(upstream, normed)) * (1.0 / width)
    return [rstd * (u - first - n * second) for u, n in zip(upstream, normed)]


def half_masks(rows):
    lane = lax.broadcasted_iota(jnp.int32, (rows, 128), 1)
    low = lane < 64
    return low, jnp.where(low, 1.0, 0.0).astype(BF), jnp.where(low, 0.0, 1.0).astype(BF)


def two_heads(x, masks):
    return jnp.concatenate([x * masks[1], x * masks[2]], axis=0)


def one_row(x, masks):
    rows = x.shape[0] // 2
    return jnp.where(masks[0], x[:rows], x[rows:])


def softmax(scores):
    shifted = jnp.exp(scores - jnp.max(scores, axis=0, keepdims=True))
    return shifted * (1.0 / jnp.sum(shifted, axis=0, keepdims=True))


def attend_back(queries, keys, values, d_context, probs, weights, masks):
    d_weights = dot_nt(values, d_context)
    mean = jnp.sum(d_weights * probs, axis=0, keepdims=True)
    d_scores = (probs * (d_weights - mean)).astype(BF)
    d_queries = one_row(dot_tn(d_scores, keys), masks)
    return d_queries, dot(d_scores, queries), dot(weights, d_context)


def axis_places():
    lon, lat = lax.axis_index("lon"), lax.axis_index("lat")
    return jnp.stack([lon >> 2, (lon >> 1) & 1, lon & 1, lat >> 1, lat & 1]).astype(jnp.int32)


def row_choice(place, rows, features, per_share, both_halves):
    r = lax.broadcasted_iota(jnp.int32, (rows, features), 0)
    col = lax.broadcasted_iota(jnp.int32, (rows, features), 1)
    low = r & (per_share - 1)
    r = r >> (per_share.bit_length() - 1)
    if both_halves:
        x_hi = (r & 1) ^ place[4]
        r = r >> 1
    else:
        x_hi = place[4]
    x_lo = (r & 1) ^ place[1]
    z = ((r >> 1) + place[3]) & 3
    core = ((r >> 3) & 1) ^ place[2]
    share = ((x_lo * 2 + core) * 8) + z * 2 + x_hi
    return jnp.where(share * per_share + low == col, 1.0, 0.0).astype(BF)


def interleave(own, far):
    return jnp.concatenate([own[:72], far[:72], own[72:], far[72:]], axis=0)


def first_rows(x):
    return jnp.concatenate([x[0:72], x[144:216]], axis=0)


def last_rows(x):
    return jnp.concatenate([x[72:144], x[216:288]], axis=0)


def fetch(sems, *pairs):
    copies = [pltpu.make_async_copy(src, dst, sems.at[i]) for i, (src, dst) in enumerate(pairs)]
    for copy in copies:
        copy.start()
    return copies


def window_forward(x, w_qkv, w_out, loads, stash, stash_out, sems):
    stores = [pltpu.make_async_copy(a, b, sems.at[i]) for i, (a, b) in enumerate(zip(stash, stash_out))]
    x_ref, qkv, ctx, prob = stash
    x_ref[...] = x.astype(BF)
    stores[0].start()
    (normed,), _ = norm_parts([x])
    normed = normed.astype(BF)
    if loads:
        loads[0].wait()
    for n in range(3):
        part = dot(normed, w_qkv[:, n * 512 : (n + 1) * 512])
        if n == 0:
            part = part * (512 // HEADS) ** (-0.5)
        qkv[:, n * 512 : (n + 1) * 512] = part.astype(BF)
    stores[1].start()
    masks = half_masks(144)
    for w in range(2):
        rows = slice(w * 144, (w + 1) * 144)
        for h in range(4):
            lanes = slice(h * 128, (h + 1) * 128)
            queries = two_heads(qkv[rows, lanes], masks)
            keys = qkv[rows, 512 + h * 128 : 512 + (h + 1) * 128]
            values = qkv[rows, 1024 + h * 128 : 1024 + (h + 1) * 128]
            weights = softmax(dot_nt(keys, queries)).astype(BF)
            prob[w * 4 + h] = weights
            ctx[rows, lanes] = one_row(dot_tn(weights, values), masks).astype(BF)
    stores[3].start()
    stores[2].start()
    if loads:
        loads[1].wait()
    return x + dot(ctx[...], w_out[...]), stores


def first_forward_kernel(
    tok_in, put_in, w_qkv_in, w_out_in, result, x_last, *refs
):
    stash_out, stash, (tok, put, w_qkv, w_out, sems, out_sems) = refs[:4], refs[4:8], refs[8:]
    loads = fetch(sems, (tok_in, tok), (put_in, put), (w_qkv_in, w_qkv), (w_out_in, w_out))
    loads[0].wait()
    loads[1].wait()
    x = dot(put[...], tok[...])
    x_last[...] = x[288:].astype(BF)
    y, stores = window_forward(x[:288], w_qkv, w_out, loads[2:], stash, stash_out, out_sems)
    result[...] = y.astype(BF)
    for store in stores:
        store.wait()


def second_forward_kernel(
    x_last_in, halo_in, put_halo_in, w_qkv_in, w_out_in, last, tail, *refs
):
    stash_out, stash, (x_last, halo, put_halo, w_qkv, w_out, sems, out_sems) = (
        refs[:4],
        refs[4:8],
        refs[8:],
    )
    loads = fetch(
        sems,
        (x_last_in, x_last),
        (halo_in, halo),
        (put_halo_in, put_halo),
        (w_qkv_in, w_qkv),
        (w_out_in, w_out),
    )
    for load in loads[:3]:
        load.wait()
    x = interleave(x_last[...].astype(F32), dot(put_halo[...], halo[...]))
    y, stores = window_forward(x, w_qkv, w_out, loads[3:], stash, stash_out, out_sems)
    last[...] = first_rows(y).astype(BF)
    tail[...] = last_rows(y).astype(BF)
    for store in stores:
        store.wait()


def cotangent_kernel(cot_own, cot_far, w_out, cot, d_ctx):
    cot[...] = interleave(cot_own[...].astype(F32), cot_far[...].astype(F32)).astype(BF)
    for n in range(2):
        lanes = slice(n * 512, (n + 1) * 512)
        d_ctx[:, lanes] = dot_nt(cot[...], w_out[lanes, :]).astype(BF)


def coarse_kernel(
    place_ref,
    body_own,
    last_own,
    tail_own,
    body_far,
    last_far,
    tail_far,
    put_body,
    put_last,
    put_tail,
    cot,
    d_ctx,
    w_merge_in,
    w_qkv_in,
    merged_ref,
    ctx_ref,
    d_qkv_ref,
    stacked_out,
    send,
    keep,
    normed_ref,
    qkv_ref,
    left_qkv,
    left_out,
    w_merge,
    w_qkv,
    sems,
    factor,
):
    loads = fetch(sems, (w_merge_in, w_merge), (w_qkv_in, w_qkv))
    place = [place_ref[i] for i in range(5)]

    def stack(body, last, tail):
        return (
            dot(put_body[...], body[...])
            + dot(put_last[...], last[...])
            + dot(put_tail[...], tail[...])
        )

    own = stack(body_own, last_own, tail_own)
    far = stack(body_far, last_far, tail_far)
    parts = [interleave(own[g * 144 : (g + 1) * 144], far[g * 144 : (g + 1) * 144]) for g in range(4)]
    for g in range(4):
        stacked_out[g] = parts[g].astype(BF)
    normed, _ = norm_parts(parts)
    loads[0].wait()
    merged = sum(dot(normed[g].astype(BF), w_merge[g * 512 : (g + 1) * 512, :]) for g in range(4))
    merged_ref[...] = merged.astype(BF)
    merged = merged_ref[...].astype(F32)
    (normed,), _ = norm_parts([merged])
    normed_ref[...] = normed.astype(BF)
    loads[1].wait()

    def project(n):
        part = dot(normed_ref[...], w_qkv[:, span(n, 512)])
        scale = jnp.where(n < 2, (1024 // HEADS2) ** (-0.5), 1.0)
        qkv_ref[:, span(n, 512)] = (part * scale).astype(BF)

    steps(6, project)
    masks = half_masks(144)
    for h in range(8):
        lanes, key_lanes, value_lanes = (slice(n * 128, (n + 1) * 128) for n in (h, h + 8, h + 16))
        for pair in range(2):
            rows = slice(pair * 144, (pair + 1) * 144)
            queries = two_heads(qkv_ref[rows, lanes], masks)
            keys = qkv_ref[rows, key_lanes]
            values = qkv_ref[rows, value_lanes]
            d_context = two_heads(d_ctx[rows, lanes], masks)
            probs = softmax(dot_nt(keys, queries))
            weights = probs.astype(BF)
            ctx_ref[rows, lanes] = one_row(dot_tn(weights, values), masks).astype(BF)
            d_queries, d_keys, d_values = attend_back(
                queries, keys, values, d_context, probs, weights, masks
            )
            d_qkv_ref[rows, lanes] = (d_queries * (1024 // HEADS2) ** (-0.5)).astype(BF)
            d_qkv_ref[rows, key_lanes] = d_keys.astype(BF)
            d_qkv_ref[rows, value_lanes] = d_values.astype(BF)

    choice = row_choice(place, 128, 256, 8, False)
    for y in range(4):
        lanes = span((place[0] + y) & 3, 256)
        block = dot_nt(choice, normed_ref[:, lanes]).astype(BF)
        other = dot_nt(choice, ctx_ref[:, lanes]).astype(BF)
        for cz in range(8):
            rows = slice((cz * 4 + y) * 16, (cz * 4 + y + 1) * 16)
            left_qkv[rows] = block[cz * 16 : (cz + 1) * 16]
            left_out[rows] = other[cz * 16 : (cz + 1) * 16]

    def grads_qkv(n):
        part = (dot(left_qkv[...], d_qkv_ref[:, span(n, 512)]) * factor).astype(BF)
        keep[:, span(n, 512)] = part[:256]
        send[:, span(n, 512)] = part[256:]

    steps(6, grads_qkv)

    def grads_out(n):
        part = (dot(left_out[...], cot[:, span(n, 512)]) * factor).astype(BF)
        keep[:, span(n + 6, 512)] = part[:256]
        send[:, span(n + 6, 512)] = part[256:]

    steps(2, grads_out)


def merge_back_kernel(
    place_ref,
    merged,
    ctx,
    d_qkv,
    stacked,
    cot,
    put_body,
    put_last,
    put_tail,
    w_qkv,
    w_merge,
    w_out,
    coarse,
    d_body,
    d_last,
    d_tail,
    send,
    keep,
    normed_ref,
    d_merged_ref,
    d_stacked_ref,
    left,
    factor,
):
    place = [place_ref[i] for i in range(5)]
    stack_normed, stack_rstd = norm_parts([stacked[g].astype(F32) for g in range(4)])
    for g in range(4):
        normed_ref[g] = stack_normed[g].astype(BF)
    d_normed = jnp.zeros((288, 1024), F32)
    for n in range(3):
        d_normed = d_normed + dot_nt(
            d_qkv[:, n * 1024 : (n + 1) * 1024], w_qkv[:, n * 1024 : (n + 1) * 1024]
        )
    d_normed = d_normed.astype(BF).astype(F32)
    (normed,), rstd = norm_parts([merged[...].astype(F32)])
    (d_input,) = norm_back([normed], rstd, [d_normed])
    d_input = cot[...].astype(F32) + d_input
    d_merged_ref[...] = d_input.astype(BF)
    d_own = first_rows(d_input).astype(BF)

    upstream = []
    for g in range(4):
        part = dot_nt(d_own, w_merge[g * 512 : (g + 1) * 512, :])
        upstream.append(part.astype(BF).astype(F32))
    own = norm_back([first_rows(n) for n in stack_normed], first_rows(stack_rstd), upstream)
    for g in range(4):
        d_stacked_ref[g * 144 : (g + 1) * 144, :] = own[g].astype(BF)
    d_tail[...] = dot(put_tail[...], d_stacked_ref[...]).astype(BF)
    d_body[...] = dot(put_body[...], d_stacked_ref[...]).astype(BF)
    d_last[...] = dot(put_last[...], d_stacked_ref[...]).astype(BF)

    choice = row_choice(place, 256, 512, 16, False)
    for y in range(4):
        block = dot_nt(choice, normed_ref[(place[0] + y) & 3])
        for cz in range(8):
            for half in range(2):
                start = cz * 32 + half * 8
                rows = jnp.concatenate([block[start : start + 8], block[start + 16 : start + 24]], axis=0)
                left[half, (cz * 4 + y) * 16 : (cz * 4 + y + 1) * 16] = rows.astype(BF)
    for n in range(4):
        columns = slice(n * 512, (n + 1) * 512)
        part = dot(left[n // 2], d_merged_ref[:, (n % 2) * 512 : (n % 2 + 1) * 512])
        part = (part * factor).astype(BF)
        keep[:, columns] = part[:256]
        send[:, columns] = part[256:]

    projected = dot(ctx[...], w_out[...])
    coarse[...] = first_rows(merged[...].astype(F32) + projected).astype(BF)


def windows_back(d_res, qkv, prob, d_ctx_ref, d_qkv_ref, w_out, first):
    d_ctx_ref[...] = dot_nt(d_res[...], w_out[...]).astype(BF)
    masks = half_masks(144)
    for w in range(2):
        rows = slice(w * 144, (w + 1) * 144)
        put = slice(first + w * 144, first + (w + 1) * 144)
        for h in range(4):
            lanes = slice(h * 128, (h + 1) * 128)
            key_lanes = slice(512 + h * 128, 512 + (h + 1) * 128)
            value_lanes = slice(1024 + h * 128, 1024 + (h + 1) * 128)
            weights = prob[w * 4 + h]
            d_queries, d_keys, d_values = attend_back(
                two_heads(qkv[rows, lanes], masks),
                qkv[rows, key_lanes],
                qkv[rows, value_lanes],
                two_heads(d_ctx_ref[rows, lanes], masks),
                weights.astype(F32),
                weights,
                masks,
            )
            d_qkv_ref[put, lanes] = (d_queries * (512 // HEADS) ** (-0.5)).astype(BF)
            d_qkv_ref[put, key_lanes] = d_keys.astype(BF)
            d_qkv_ref[put, value_lanes] = d_values.astype(BF)


def input_back(d_res, d_qkv, x, w_qkv):
    (normed,), rstd = norm_parts([x[...].astype(F32)])
    d_normed = dot_nt(d_qkv[...], w_qkv[...]).astype(BF).astype(F32)
    (d_input,) = norm_back([normed], rstd, [d_normed])
    return d_res[...].astype(F32) + d_input


def first_back_kernel(d_res, x, qkv, prob, w_qkv, w_out, d_qkv, d_x, d_ctx_ref):
    windows_back(d_res, qkv, prob, d_ctx_ref, d_qkv, w_out, 0)
    d_x[...] = input_back(d_res, d_qkv, x, w_qkv).astype(BF)


def second_back_kernel(
    place_ref,
    d_last,
    d_tail,
    d_first,
    d_qkv_first,
    x_first,
    x_second,
    ctx_first,
    ctx_second,
    qkv,
    prob,
    w_out,
    d_res_out,
    d_qkv_out,
    send,
    keep,
    normed_ref,
    ctx_ref,
    d_ctx_ref,
    d_res_ref,
    d_qkv_ref,
    left_qkv,
    left_out,
    factor,
):
    place = [place_ref[i] for i in range(5)]
    d_res_out[...] = interleave(d_last[...].astype(F32), d_tail[...].astype(F32)).astype(BF)
    windows_back(d_res_out, qkv, prob, d_ctx_ref, d_qkv_ref, w_out, 288)
    d_qkv_out[...] = d_qkv_ref[288:576]
    for half, (x, ctx, d_res) in enumerate(
        ((x_first, ctx_first, d_first), (x_second, ctx_second, d_res_out))
    ):
        rows = slice(half * 288, (half + 1) * 288)
        (normed,), _ = norm_parts([x[...].astype(F32)])
        normed_ref[rows] = normed.astype(BF)
        ctx_ref[rows] = ctx[...]
        d_res_ref[rows] = d_res[...]
    d_qkv_ref[0:288] = d_qkv_first[...]
    choice = row_choice(place, 128, 128, 4, True)
    for y in range(4):
        lanes = span((place[0] + y) & 3, 128)
        block = dot_nt(choice, normed_ref[:, lanes]).astype(BF)
        other = dot_nt(choice, ctx_ref[:, lanes]).astype(BF)
        for cz in range(8):
            rows = slice((cz * 4 + y) * 16, (cz * 4 + y + 1) * 16)
            left_qkv[rows] = block[cz * 16 : (cz + 1) * 16]
            left_out[rows] = other[cz * 16 : (cz + 1) * 16]
    for n in range(4):
        columns = slice(n * 512, (n + 1) * 512)
        if n < 3:
            part = dot(left_qkv[...], d_qkv_ref[:, columns])
        else:
            part = dot(left_out[...], d_res_ref[...])
        part = (part * factor).astype(BF)
        keep[:, columns] = part[:256]
        send[:, columns] = part[256:]


def last_back_kernel(d_res, d_qkv, x, w_qkv, d_last, d_tail):
    d_input = input_back(d_res, d_qkv, x, w_qkv)
    d_last[...] = first_rows(d_input).astype(BF)
    d_tail[...] = last_rows(d_input).astype(BF)


def place_result_kernel(body, last, tail, put_body, put_last, put_tail, out):
    out[...] = (
        dot(put_body[...], body[...]) + dot(put_last[...], last[...]) + dot(put_tail[...], tail[...])
    ).astype(BF)


def call(kernel, outs, scratch=(), scalars=0, far=(), far_outs=(), us=1, room=4, after=(), limit=None, through=()):
    def run(*args):
        in_specs = [
            pl.BlockSpec(
                memory_space=pltpu.SMEM if i < scalars else pltpu.HBM if i in far else pltpu.VMEM
            )
            for i in range(len(args))
        ]
        out_specs = [
            pl.BlockSpec(memory_space=pltpu.HBM if i in far_outs else pltpu.VMEM)
            for i in range(len(outs))
        ]
        held = sum(a.size * a.dtype.itemsize for i, a in enumerate(args) if i not in far)
        shapes = [o for i, o in enumerate(outs) if i not in far_outs] + list(scratch)
        held += sum(int(np.prod(s)) * jnp.dtype(d).itemsize for s, d in shapes)
        scratch_shapes = [pltpu.VMEM(shape, dtype) for shape, dtype in scratch]
        for moved in (far, far_outs):
            if moved:
                scratch_shapes.append(pltpu.SemaphoreType.DMA((len(moved),)))
        body = kernel
        idle = len(through) + len(after)
        if idle:

            def body(*refs):
                refs = refs[: len(args)] + refs[len(args) + idle :]
                results = len(args) + len(outs)
                kernel(*refs[:results], *refs[results + len(through) :])

        return pl.pallas_call(
            body,
            out_shape=[jax.ShapeDtypeStruct(shape, dtype) for shape, dtype in outs]
            + [jax.ShapeDtypeStruct(a.shape, a.dtype) for a in through],
            in_specs=in_specs + [pl.BlockSpec(memory_space=pl.ANY)] * idle,
            out_specs=out_specs + [pl.BlockSpec(memory_space=pl.ANY)] * len(through),
            input_output_aliases={len(args) + i: len(outs) + i for i in range(len(through))},
            scratch_shapes=scratch_shapes,
            cost_estimate=pl.CostEstimate(
                flops=int(us * 1e9), bytes_accessed=int(us * 3e6), transcendentals=0
            ),
            compiler_params=pltpu.CompilerParams(
                vmem_limit_bytes=limit * MIB if limit else int(held * 1.15) + room * MIB
            ),
        )(*args, *through, *after)

    return run


def route(move):
    pairs = []
    for source in range(128):
        lon, lat = divmod(source, 8)
        y, x_lo, core, z, x_hi = move(lon >> 2, (lon >> 1) & 1, lon & 1, lat >> 1, lat & 1)
        pairs.append((source, (((y & 3) * 2 + x_lo) * 2 + core) * 8 + (z & 3) * 2 + x_hi))
    return pairs


def groups():
    return [
        [((y * 2 + x_lo) * 2 + core) * 8 + z * 2 + x_hi for y in range(4) for x_lo in range(2) for x_hi in range(2)]
        for core in range(2)
        for z in range(4)
    ]


def send_core(x):
    return lax.ppermute(x, ("lon", "lat"), route(lambda y, xl, c, z, xh: (y, xl, 1 - c, z, xh)))


def send_z(x, d):
    return lax.ppermute(x, ("lon", "lat"), route(lambda y, xl, c, z, xh: (y, xl, c, z + d, xh)))


def send_y(x, d):
    return lax.ppermute(x, ("lon", "lat"), route(lambda y, xl, c, z, xh: (y + d, xl, c, z, xh)))


def send_x_lo(x):
    return lax.ppermute(x, ("lon", "lat"), route(lambda y, xl, c, z, xh: (y, 1 - xl, c, z, xh)))


def send_lon(x, step, partner):
    pairs = []
    for lon in range(16):
        for lat in range(8):
            pairs.append((lon * 8 + lat, (lon + step) % 16 * 8 + (lat ^ partner)))
    return lax.ppermute(x, ("lon", "lat"), pairs)


def add(*refs):
    return sum(r.astype(F32) for r in refs)


def wide_split_kernel(keep_a, got_a, keep_m, got_m, *pieces):
    def by_z(d, o):
        return (
            add(keep_a[d, o, :, :2048], got_a[d, o, :, :2048]).astype(BF),
            add(keep_m[d, o, :, :1024], got_m[d, o, :, :1024]).astype(BF),
        )

    def by_y(d, o):
        return (
            add(keep_a[o, d, :, 2048:], got_a[o, d, :, 2048:]).astype(BF),
            add(keep_m[o, d, :, 1024:], got_m[o, d, :, 1024:]).astype(BF),
        )

    for ring, block in ((pieces[:5], by_z), (pieces[5:], by_y)):
        for d, ref in ((0, ring[0]), (1, ring[1]), (3, ring[2])):
            for o in range(4):
                ref[o, :, :2048], ref[o, :, 2048:] = block(d, o)
        for o in range(4):
            ref = ring[3 + o // 2]
            ref[o % 2, :, :2048], ref[o % 2, :, 2048:] = block(2, o)


def wide_pass_kernel(*refs):
    for ring in range(2):
        up, down, from_below, from_above, up_out, down_out = refs[ring * 4 : ring * 4 + 4] + refs[8 + ring * 2 : 10 + ring * 2]
        for o in range(4):
            if o < 2:
                up_out[o] = add(up[o], from_below[o]).astype(BF)
                down_out[o] = down[o]
            else:
                up_out[o] = up[o]
                down_out[o] = add(down[o], from_above[o - 2]).astype(BF)


def wide_sum_kernel(*refs):
    first, last, by_y, by_z = refs[:3], refs[3:6], refs[6:10], refs[10]
    for d in range(4):
        by_y[d][...] = add(*(r[d] for r in first)).astype(BF)
        by_z[d] = add(*(r[d] for r in last)).astype(BF)


def joint_split_kernel(last, keep, got, *to_z):
    for d in range(4):
        for y in range(4):
            to_z[d][:, y * 2048 : (y + 1) * 2048] = add(keep[d, y], got[d, y]).astype(BF)
        to_z[d][:, 8192:] = last[d]


def joint_sum_kernel(place_ref, *refs):
    from_z, from_y, fine, wide_keep, wide_send = refs[:4], refs[4:8], refs[8], refs[9], refs[10]
    for d in range(4):
        y = (place_ref[0] + d) & 3
        sums = add(*(r[:, d * 2048 : (d + 1) * 2048] for r in from_z))
        for x_lo in range(2):
            for x_hi in range(2):
                part = sums[x_lo * 8 + x_hi * 4 : x_lo * 8 + x_hi * 4 + 4]
                part = jnp.concatenate([part[:, q * 512 : (q + 1) * 512] for q in range(4)], axis=0)
                device = y * 4 + (place_ref[1] ^ x_lo) * 2 + (place_ref[4] ^ x_hi)
                fine[span(device, 16), :] = part.astype(BF)
    first = add(*(r[...] for r in from_y))
    last = add(*(r[:, 8192:] for r in from_z))
    for wide, rows in ((wide_keep, slice(0, 8)), (wide_send, slice(8, 16))):
        wide[:, :3072] = first[rows].astype(BF)
        wide[:, 3072:] = last[rows].astype(BF)


def shares_kernel(fine_got, wide_keep, wide_got, fine_qkv, fine_out, merge, coarse_qkv, coarse_out):
    fine = add(*(fine_got[d * 16 : (d + 1) * 16] for d in range(16)))
    for q in range(3):
        fine_qkv[:, q * 512 : (q + 1) * 512] = fine[q * 4 : (q + 1) * 4]
    fine_out[...] = fine[12:]
    wide = add(wide_keep[...], wide_got[...])
    coarse_qkv[:, :2048] = wide[:, :2048]
    coarse_qkv[:, 2048:] = wide[:, 3072:4096]
    coarse_out[...] = wide[:, 4096:5120]
    merge[0:8] = wide[:, 2048:3072]
    merge[8:16] = wide[:, 5120:6144]


def blocks(x):
    return x.reshape(4, 4, 16, x.shape[1])


def local(tokens, cotangent, fine_qkv, fine_out, merge_weight, coarse_qkv, coarse_out):
    factor = (144 * lax.axis_size("lon") * lax.axis_size("lat")) ** (-0.5)
    place = axis_places()
    put_own, put_halo = (jnp.asarray(a, BF) for a in place_tokens())
    stack = place_stacked()
    unstack = [jnp.asarray(a.T, BF) for a in stack]
    stack = [jnp.asarray(a, BF) for a in stack]
    result = [jnp.asarray(a, BF) for a in place_result()]

    tok = tokens.transpose(0, 2, 1, 3)
    halo = send_lon(tok[:, :, :8], -1, 0).reshape(192, 512)
    cot_own = cotangent.reshape(144, 1024)
    cot_far = send_lon(cot_own, 0, 1)

    stash = [((288, 512), BF), ((288, 1536), BF), ((288, 512), BF), ((8, 144, 288), BF)]
    fine_weights = [((512, 1536), BF), ((512, 512), BF)]
    body, x_last, x_first, qkv_first, ctx_first, prob_first = call(
        first_forward_kernel,
        [((288, 512), BF), ((144, 512), BF)] + stash,
        stash + [((576, 512), BF), ((432, 576), BF)] + fine_weights,
        far=(0, 1, 2, 3),
        far_outs=(2, 3, 4, 5),
        us=6,
        limit=60,
    )(tok.reshape(576, 512), put_own, fine_qkv, fine_out)
    body_far = send_lon(body, 0, 1)
    last, tail, x_second, qkv_second, ctx_second, prob_second = call(
        second_forward_kernel,
        [((144, 512), BF)] * 2 + stash,
        stash + [((144, 512), BF), ((192, 512), BF), ((144, 192), BF)] + fine_weights,
        far=(0, 1, 2, 3, 4),
        far_outs=(2, 3, 4, 5),
        us=6,
        limit=60,
        after=(cot_far,),
    )(x_last, halo, put_halo, fine_qkv, fine_out)
    tail_own = send_lon(tail, 1, 0)
    tail_far = send_lon(tail, 1, 1)
    last_far = send_lon(last, 0, 1)
    cot, d_ctx = call(cotangent_kernel, [((288, 1024), BF)] * 2, us=3)(cot_own, cot_far, coarse_out)

    merged, ctx, d_qkv, stacked, send_a, keep_a = call(
        functools.partial(coarse_kernel, factor=factor),
        [
            ((288, 1024), BF),
            ((288, 1024), BF),
            ((288, 3072), BF),
            ((4, 288, 512), BF),
            ((256, 4096), BF),
            ((256, 4096), BF),
        ],
        [
            ((288, 1024), BF),
            ((288, 3072), BF),
            ((512, 288), BF),
            ((512, 288), BF),
            ((2048, 1024), BF),
            ((1024, 3072), BF),
        ],
        scalars=1,
        far=(12, 13),
        us=20,
        room=8,
    )(
        place,
        body,
        last,
        tail_own,
        body_far,
        last_far,
        tail_far,
        *stack,
        cot,
        d_ctx,
        merge_weight,
        coarse_qkv,
    )
    got_a = send_core(send_a)

    coarse, d_first, d_last, d_tail, send_m, keep_m = call(
        functools.partial(merge_back_kernel, factor=factor),
        [
            ((144, 1024), BF),
            ((288, 512), BF),
            ((144, 512), BF),
            ((144, 512), BF),
            ((256, 2048), BF),
            ((256, 2048), BF),
        ],
        [
            ((4, 288, 512), BF),
            ((288, 1024), BF),
            ((576, 512), BF),
            ((2, 512, 288), BF),
        ],
        scalars=1,
        us=12,
        room=8,
    )(place, merged, ctx, d_qkv, stacked, cot, *unstack, coarse_qkv, merge_weight, coarse_out)
    d_tail = send_lon(d_tail, -1, 0)
    got_m = send_core(send_m)

    ring_shapes = ([((4, 16, 3072), BF)] * 3 + [((2, 16, 3072), BF)] * 2) * 2
    pieces = call(wide_split_kernel, ring_shapes, us=4)(
        blocks(keep_a), blocks(got_a), blocks(keep_m), blocks(got_m)
    )
    wide_z, wide_y = pieces[:5], pieces[5:]
    passed = (
        send_z(wide_z[3], 1),
        send_z(wide_z[4], -1),
        send_y(wide_y[3], 1),
        send_y(wide_y[4], -1),
    )

    d_qkv_first, d_x_first = call(
        first_back_kernel,
        [((288, 1536), BF), ((288, 512), BF)],
        [((288, 512), BF)],
        us=8,
        after=(pieces[0],),
    )(d_first, x_first, qkv_first, prob_first, fine_qkv, fine_out)

    up_z, down_z, up_y, down_y = call(
        wide_pass_kernel, [((4, 16, 3072), BF)] * 4, us=2, after=(d_qkv_first,)
    )(wide_z[1], wide_z[2], *passed[:2], wide_y[1], wide_y[2], *passed[2:])
    wide_z = (wide_z[0], send_z(up_z, 1), send_z(down_z, -1))
    wide_y = (wide_y[0], send_y(up_y, 1), send_y(down_y, -1))

    d_res, d_qkv_second, send_f, keep_f = call(
        functools.partial(second_back_kernel, factor=factor),
        [((288, 512), BF), ((288, 1536), BF), ((256, 2048), BF), ((256, 2048), BF)],
        [
            ((576, 512), BF),
            ((576, 512), BF),
            ((288, 512), BF),
            ((576, 512), BF),
            ((576, 1536), BF),
            ((512, 576), BF),
            ((512, 576), BF),
        ],
        scalars=1,
        us=10,
        after=(up_z,),
    )(
        place,
        d_last,
        d_tail,
        d_first,
        d_qkv_first,
        x_first,
        x_second,
        ctx_first,
        ctx_second,
        qkv_second,
        prob_second,
        fine_out,
    )
    *wide_first, wide_last, send_f = call(
        wide_sum_kernel,
        [((16, 3072), BF)] * 4 + [((4, 16, 3072), BF)],
        us=2,
        through=(send_f,),
    )(*wide_z, *wide_y)
    got_f = send_core(send_f)
    d_x_last, d_x_tail = call(last_back_kernel, [((144, 512), BF)] * 2, us=2)(
        d_res, d_qkv_second, x_second, fine_qkv
    )
    d_x_tail = send_lon(d_x_tail, 1, 0)
    to_z = call(joint_split_kernel, [((16, 11264), BF)] * 4, us=1, after=(d_x_last,))(
        wide_last, blocks(keep_f), blocks(got_f)
    )
    from_z = [to_z[0]] + [send_z(to_z[d], d) for d in (1, 2, 3)]
    from_y = [wide_first[0]] + [send_y(wide_first[d], d) for d in (1, 2, 3)]
    (d_tokens,) = call(place_result_kernel, [((576, 512), BF)], us=2)(
        d_x_first, d_x_last, d_x_tail, *result
    )
    fine, wide_keep, wide_send = call(
        joint_sum_kernel,
        [((256, 512), BF)] + [((8, 6144), BF)] * 2,
        scalars=1,
        after=(d_tokens,),
    )(place, *from_z, *from_y)
    wide_got = send_x_lo(wide_send)
    fine = lax.all_to_all(fine, ("lon", "lat"), 0, 0, axis_index_groups=groups(), tiled=True)
    shares = call(
        shares_kernel,
        [
            ((4, 1536), F32),
            ((4, 512), F32),
            ((16, 1024), F32),
            ((8, 3072), F32),
            ((8, 1024), F32),
        ],
    )(fine, wide_keep, wide_got)
    return (
        coarse.reshape(4, 12, 3, 1024),
        d_tokens.reshape(4, 6, 24, 512).transpose(0, 2, 1, 3),
        *shares,
    )


def solution(mesh):
    grid_spec = P(None, "lon", "lat", None)
    rows_spec = P(("lon", "lat"), None)
    return jax.shard_map(
        local,
        mesh=mesh,
        in_specs=(grid_spec, grid_spec, P(), P(), P(), P(), P()),
        out_specs=(grid_spec, grid_spec) + (rows_spec,) * 5,
        check_vma=False,
    )
```

```python
import functools

import jax
import jax.numpy as jnp
import numpy as np
from jax import lax
from jax.experimental import pallas as pl
from jax.experimental.pallas import tpu as pltpu
from jax.sharding import PartitionSpec as P

HEADS = 8
HEADS2 = 16
NORM_EPS = 1e-05
BF = jnp.bfloat16
F32 = jnp.float32
VMEM = pl.BlockSpec(memory_space=pltpu.VMEM)
MIB = 1024 * 1024


def place_tokens():
    own = np.zeros((432, 576), np.float32)
    halo = np.zeros((144, 192), np.float32)
    for pair in range(2):
        for quarter in range(4):
            for level in range(2):
                for lat in range(6):
                    for lon in range(6):
                        inner = level * 36 + lat * 6 + lon
                        line = (2 * pair + level) * 6 + lat
                        if quarter < 2:
                            own[pair * 144 + quarter * 72 + inner, line * 24 + 6 * quarter + lon + 6] = 1
                        elif quarter == 2:
                            own[288 + pair * 72 + inner, line * 24 + lon + 18] = 1
                        else:
                            halo[pair * 72 + inner, line * 8 + lon] = 1
    return own, halo


def place_stacked():
    body = np.zeros((576, 288), np.float32)
    last = np.zeros((576, 144), np.float32)
    tail = np.zeros((576, 144), np.float32)
    for a in range(2):
        for b in range(2):
            for pair in range(2):
                for level in range(2):
                    for i in range(12):
                        for j in range(3):
                            row = (a * 2 + b) * 144 + pair * 72 + level * 36 + i * 3 + j
                            quarter, lon, lat = i // 3, 2 * (i % 3) + a, 2 * j + b
                            inner = level * 36 + lat * 6 + lon
                            if quarter == 0:
                                tail[row, pair * 72 + inner] = 1
                            elif quarter == 3:
                                last[row, pair * 72 + inner] = 1
                            else:
                                body[row, pair * 144 + (quarter - 1) * 72 + inner] = 1
    return body, last, tail


def place_result():
    body = np.zeros((576, 288), np.float32)
    last = np.zeros((576, 144), np.float32)
    tail = np.zeros((576, 144), np.float32)
    for level in range(4):
        for lat in range(6):
            for lon in range(24):
                row = (level * 6 + lat) * 24 + lon
                inner = (level % 2) * 36 + lat * 6 + lon % 6
                if lon < 6:
                    tail[row, (level // 2) * 72 + inner] = 1
                elif lon >= 18:
                    last[row, (level // 2) * 72 + inner] = 1
                else:
                    body[row, (level // 2) * 144 + (lon // 6 - 1) * 72 + inner] = 1
    return body, last, tail


def dot(a, b):
    return lax.dot_general(a, b, (((1,), (0,)), ((), ())), preferred_element_type=F32)


def dot_nt(a, b):
    return lax.dot_general(a, b, (((1,), (1,)), ((), ())), preferred_element_type=F32)


def dot_tn(a, b):
    return lax.dot_general(a, b, (((0,), (0,)), ((), ())), preferred_element_type=F32)


def steps(count, body):
    lax.fori_loop(0, count, lambda i, carry: (body(i), carry)[1], 0)


def span(i, size):
    return pl.ds(pl.multiple_of(i * size, size), size)


def total(x):
    return jnp.sum(x, axis=-1, keepdims=True)


def norm_parts(parts):
    width = sum(p.shape[1] for p in parts)
    mean = sum(total(p) for p in parts) * (1.0 / width)
    centred = [p - mean for p in parts]
    rstd = lax.rsqrt(sum(total(c * c) for c in centred) * (1.0 / width) + NORM_EPS)
    return [c * rstd for c in centred], rstd


def norm_back(normed, rstd, upstream):
    width = sum(p.shape[1] for p in normed)
    first = sum(total(u) for u in upstream) * (1.0 / width)
    second = sum(total(u * n) for u, n in zip(upstream, normed)) * (1.0 / width)
    return [rstd * (u - first - n * second) for u, n in zip(upstream, normed)]


def half_masks(rows):
    lane = lax.broadcasted_iota(jnp.int32, (rows, 128), 1)
    low = lane < 64
    return low, jnp.where(low, 1.0, 0.0).astype(BF), jnp.where(low, 0.0, 1.0).astype(BF)


def two_heads(x, masks):
    return jnp.concatenate([x * masks[1], x * masks[2]], axis=0)


def one_row(x, masks):
    rows = x.shape[0] // 2
    return jnp.where(masks[0], x[:rows], x[rows:])


def softmax(scores):
    shifted = jnp.exp(scores - jnp.max(scores, axis=0, keepdims=True))
    return shifted * (1.0 / jnp.sum(shifted, axis=0, keepdims=True))


def attend_back(queries, keys, values, d_context, probs, weights, masks):
    d_weights = dot_nt(values, d_context)
    mean = jnp.sum(d_weights * probs, axis=0, keepdims=True)
    d_scores = (probs * (d_weights - mean)).astype(BF)
    d_queries = one_row(dot_tn(d_scores, keys), masks)
    return d_queries, dot(d_scores, queries), dot(weights, d_context)


def axis_places():
    lon, lat = lax.axis_index("lon"), lax.axis_index("lat")
    return jnp.stack([lon >> 2, (lon >> 1) & 1, lon & 1, lat >> 1, lat & 1]).astype(jnp.int32)


def row_choice(place, rows, features, per_share, both_halves):
    r = lax.broadcasted_iota(jnp.int32, (rows, features), 0)
    col = lax.broadcasted_iota(jnp.int32, (rows, features), 1)
    low = r & (per_share - 1)
    r = r >> (per_share.bit_length() - 1)
    if both_halves:
        x_hi = (r & 1) ^ place[4]
        r = r >> 1
    else:
        x_hi = place[4]
    x_lo = (r & 1) ^ place[1]
    z = ((r >> 1) + place[3]) & 3
    core = ((r >> 3) & 1) ^ place[2]
    share = ((x_lo * 2 + core) * 8) + z * 2 + x_hi
    return jnp.where(share * per_share + low == col, 1.0, 0.0).astype(BF)


def interleave(own, far):
    return jnp.concatenate([own[:72], far[:72], own[72:], far[72:]], axis=0)


def first_rows(x):
    return jnp.concatenate([x[0:72], x[144:216]], axis=0)


def last_rows(x):
    return jnp.concatenate([x[72:144], x[216:288]], axis=0)


def fetch(sems, *pairs):
    copies = [pltpu.make_async_copy(src, dst, sems.at[i]) for i, (src, dst) in enumerate(pairs)]
    for copy in copies:
        copy.start()
    return copies


def window_forward(x, w_qkv, w_out, loads, stash, stash_out, sems):
    stores = [pltpu.make_async_copy(a, b, sems.at[i]) for i, (a, b) in enumerate(zip(stash, stash_out))]
    x_ref, qkv, ctx, prob = stash
    x_ref[...] = x.astype(BF)
    stores[0].start()
    (normed,), _ = norm_parts([x])
    normed = normed.astype(BF)
    if loads:
        loads[0].wait()
    for n in range(3):
        part = dot(normed, w_qkv[:, n * 512 : (n + 1) * 512])
        if n == 0:
            part = part * (512 // HEADS) ** (-0.5)
        qkv[:, n * 512 : (n + 1) * 512] = part.astype(BF)
    stores[1].start()
    masks = half_masks(144)
    for w in range(2):
        rows = slice(w * 144, (w + 1) * 144)
        for h in range(4):
            lanes = slice(h * 128, (h + 1) * 128)
            queries = two_heads(qkv[rows, lanes], masks)
            keys = qkv[rows, 512 + h * 128 : 512 + (h + 1) * 128]
            values = qkv[rows, 1024 + h * 128 : 1024 + (h + 1) * 128]
            weights = softmax(dot_nt(keys, queries)).astype(BF)
            prob[w * 4 + h] = weights
            ctx[rows, lanes] = one_row(dot_tn(weights, values), masks).astype(BF)
    stores[3].start()
    stores[2].start()
    if loads:
        loads[1].wait()
    return x + dot(ctx[...], w_out[...]), stores


def first_forward_kernel(
    tok_in, put_in, w_qkv_in, w_out_in, result, x_last, *refs
):
    stash_out, stash, (tok, put, w_qkv, w_out, sems, out_sems) = refs[:4], refs[4:8], refs[8:]
    loads = fetch(sems, (tok_in, tok), (put_in, put), (w_qkv_in, w_qkv), (w_out_in, w_out))
    loads[0].wait()
    loads[1].wait()
    x = dot(put[...], tok[...])
    x_last[...] = x[288:].astype(BF)
    y, stores = window_forward(x[:288], w_qkv, w_out, loads[2:], stash, stash_out, out_sems)
    result[...] = y.astype(BF)
    for store in stores:
        store.wait()


def second_forward_kernel(
    x_last_in, halo_in, put_halo_in, w_qkv_in, w_out_in, last, tail, *refs
):
    stash_out, stash, (x_last, halo, put_halo, w_qkv, w_out, sems, out_sems) = (
        refs[:4],
        refs[4:8],
        refs[8:],
    )
    loads = fetch(
        sems,
        (x_last_in, x_last),
        (halo_in, halo),
        (put_halo_in, put_halo),
        (w_qkv_in, w_qkv),
        (w_out_in, w_out),
    )
    for load in loads[:3]:
        load.wait()
    x = interleave(x_last[...].astype(F32), dot(put_halo[...], halo[...]))
    y, stores = window_forward(x, w_qkv, w_out, loads[3:], stash, stash_out, out_sems)
    last[...] = first_rows(y).astype(BF)
    tail[...] = last_rows(y).astype(BF)
    for store in stores:
        store.wait()


def cotangent_kernel(cot_own, cot_far, w_out, cot, d_ctx):
    cot[...] = interleave(cot_own[...].astype(F32), cot_far[...].astype(F32)).astype(BF)
    for n in range(2):
        lanes = slice(n * 512, (n + 1) * 512)
        d_ctx[:, lanes] = dot_nt(cot[...], w_out[lanes, :]).astype(BF)


def coarse_kernel(
    place_ref,
    body_own,
    last_own,
    tail_own,
    body_far,
    last_far,
    tail_far,
    put_body,
    put_last,
    put_tail,
    cot,
    d_ctx,
    w_merge_in,
    w_qkv_in,
    merged_ref,
    ctx_ref,
    d_qkv_ref,
    stacked_out,
    send,
    keep,
    normed_ref,
    qkv_ref,
    left_qkv,
    left_out,
    w_merge,
    w_qkv,
    sems,
    factor,
):
    loads = fetch(sems, (w_merge_in, w_merge), (w_qkv_in, w_qkv))
    place = [place_ref[i] for i in range(5)]

    def stack(body, last, tail):
        return (
            dot(put_body[...], body[...])
            + dot(put_last[...], last[...])
            + dot(put_tail[...], tail[...])
        )

    own = stack(body_own, last_own, tail_own)
    far = stack(body_far, last_far, tail_far)
    parts = [interleave(own[g * 144 : (g + 1) * 144], far[g * 144 : (g + 1) * 144]) for g in range(4)]
    for g in range(4):
        stacked_out[g] = parts[g].astype(BF)
    normed, _ = norm_parts(parts)
    loads[0].wait()
    merged = sum(dot(normed[g].astype(BF), w_merge[g * 512 : (g + 1) * 512, :]) for g in range(4))
    merged_ref[...] = merged.astype(BF)
    merged = merged_ref[...].astype(F32)
    (normed,), _ = norm_parts([merged])
    normed_ref[...] = normed.astype(BF)
    loads[1].wait()

    def project(n):
        part = dot(normed_ref[...], w_qkv[:, span(n, 512)])
        scale = jnp.where(n < 2, (1024 // HEADS2) ** (-0.5), 1.0)
        qkv_ref[:, span(n, 512)] = (part * scale).astype(BF)

    steps(6, project)
    masks = half_masks(144)
    for h in range(8):
        lanes, key_lanes, value_lanes = (slice(n * 128, (n + 1) * 128) for n in (h, h + 8, h + 16))
        for pair in range(2):
            rows = slice(pair * 144, (pair + 1) * 144)
            queries = two_heads(qkv_ref[rows, lanes], masks)
            keys = qkv_ref[rows, key_lanes]
            values = qkv_ref[rows, value_lanes]
            d_context = two_heads(d_ctx[rows, lanes], masks)
            probs = softmax(dot_nt(keys, queries))
            weights = probs.astype(BF)
            ctx_ref[rows, lanes] = one_row(dot_tn(weights, values), masks).astype(BF)
            d_queries, d_keys, d_values = attend_back(
                queries, keys, values, d_context, probs, weights, masks
            )
            d_qkv_ref[rows, lanes] = (d_queries * (1024 // HEADS2) ** (-0.5)).astype(BF)
            d_qkv_ref[rows, key_lanes] = d_keys.astype(BF)
            d_qkv_ref[rows, value_lanes] = d_values.astype(BF)

    choice = row_choice(place, 128, 256, 8, False)
    for y in range(4):
        lanes = span((place[0] + y) & 3, 256)
        block = dot_nt(choice, normed_ref[:, lanes]).astype(BF)
        other = dot_nt(choice, ctx_ref[:, lanes]).astype(BF)
        for cz in range(8):
            rows = slice((cz * 4 + y) * 16, (cz * 4 + y + 1) * 16)
            left_qkv[rows] = block[cz * 16 : (cz + 1) * 16]
            left_out[rows] = other[cz * 16 : (cz + 1) * 16]

    def grads_qkv(n):
        part = (dot(left_qkv[...], d_qkv_ref[:, span(n, 512)]) * factor).astype(BF)
        keep[:, span(n, 512)] = part[:256]
        send[:, span(n, 512)] = part[256:]

    steps(6, grads_qkv)

    def grads_out(n):
        part = (dot(left_out[...], cot[:, span(n, 512)]) * factor).astype(BF)
        keep[:, span(n + 6, 512)] = part[:256]
        send[:, span(n + 6, 512)] = part[256:]

    steps(2, grads_out)


def merge_back_kernel(
    place_ref,
    merged,
    ctx,
    d_qkv,
    stacked,
    cot,
    put_body,
    put_last,
    put_tail,
    w_qkv,
    w_merge,
    w_out,
    coarse,
    d_body,
    d_last,
    d_tail,
    send,
    keep,
    normed_ref,
    d_merged_ref,
    d_stacked_ref,
    left,
    factor,
):
    place = [place_ref[i] for i in range(5)]
    stack_normed, stack_rstd = norm_parts([stacked[g].astype(F32) for g in range(4)])
    for g in range(4):
        normed_ref[g] = stack_normed[g].astype(BF)
    d_normed = jnp.zeros((288, 1024), F32)
    for n in range(3):
        d_normed = d_normed + dot_nt(
            d_qkv[:, n * 1024 : (n + 1) * 1024], w_qkv[:, n * 1024 : (n + 1) * 1024]
        )
    d_normed = d_normed.astype(BF).astype(F32)
    (normed,), rstd = norm_parts([merged[...].astype(F32)])
    (d_input,) = norm_back([normed], rstd, [d_normed])
    d_input = cot[...].astype(F32) + d_input
    d_merged_ref[...] = d_input.astype(BF)
    d_own = first_rows(d_input).astype(BF)

    upstream = []
    for g in range(4):
        part = dot_nt(d_own, w_merge[g * 512 : (g + 1) * 512, :])
        upstream.append(part.astype(BF).astype(F32))
    own = norm_back([first_rows(n) for n in stack_normed], first_rows(stack_rstd), upstream)
    for g in range(4):
        d_stacked_ref[g * 144 : (g + 1) * 144, :] = own[g].astype(BF)
    d_tail[...] = dot(put_tail[...], d_stacked_ref[...]).astype(BF)
    d_body[...] = dot(put_body[...], d_stacked_ref[...]).astype(BF)
    d_last[...] = dot(put_last[...], d_stacked_ref[...]).astype(BF)

    choice = row_choice(place, 256, 512, 16, False)
    for y in range(4):
        block = dot_nt(choice, normed_ref[(place[0] + y) & 3])
        for cz in range(8):
            for half in range(2):
                start = cz * 32 + half * 8
                rows = jnp.concatenate([block[start : start + 8], block[start + 16 : start + 24]], axis=0)
                left[half, (cz * 4 + y) * 16 : (cz * 4 + y + 1) * 16] = rows.astype(BF)
    for n in range(4):
        columns = slice(n * 512, (n + 1) * 512)
        part = dot(left[n // 2], d_merged_ref[:, (n % 2) * 512 : (n % 2 + 1) * 512])
        part = (part * factor).astype(BF)
        keep[:, columns] = part[:256]
        send[:, columns] = part[256:]

    projected = dot(ctx[...], w_out[...])
    coarse[...] = first_rows(merged[...].astype(F32) + projected).astype(BF)


def windows_back(d_res, qkv, prob, d_ctx_ref, d_qkv_ref, w_out, first):
    d_ctx_ref[...] = dot_nt(d_res[...], w_out[...]).astype(BF)
    masks = half_masks(144)
    for w in range(2):
        rows = slice(w * 144, (w + 1) * 144)
        put = slice(first + w * 144, first + (w + 1) * 144)
        for h in range(4):
            lanes = slice(h * 128, (h + 1) * 128)
            key_lanes = slice(512 + h * 128, 512 + (h + 1) * 128)
            value_lanes = slice(1024 + h * 128, 1024 + (h + 1) * 128)
            weights = prob[w * 4 + h]
            d_queries, d_keys, d_values = attend_back(
                two_heads(qkv[rows, lanes], masks),
                qkv[rows, key_lanes],
                qkv[rows, value_lanes],
                two_heads(d_ctx_ref[rows, lanes], masks),
                weights.astype(F32),
                weights,
                masks,
            )
            d_qkv_ref[put, lanes] = (d_queries * (512 // HEADS) ** (-0.5)).astype(BF)
            d_qkv_ref[put, key_lanes] = d_keys.astype(BF)
            d_qkv_ref[put, value_lanes] = d_values.astype(BF)


def input_back(d_res, d_qkv, x, w_qkv):
    (normed,), rstd = norm_parts([x[...].astype(F32)])
    d_normed = dot_nt(d_qkv[...], w_qkv[...]).astype(BF).astype(F32)
    (d_input,) = norm_back([normed], rstd, [d_normed])
    return d_res[...].astype(F32) + d_input


def first_back_kernel(d_res, x, qkv, prob, w_qkv, w_out, d_qkv, d_x, d_ctx_ref):
    windows_back(d_res, qkv, prob, d_ctx_ref, d_qkv, w_out, 0)
    d_x[...] = input_back(d_res, d_qkv, x, w_qkv).astype(BF)


def second_back_kernel(
    place_ref,
    d_last,
    d_tail,
    d_first,
    d_qkv_first,
    x_first,
    x_second,
    ctx_first,
    ctx_second,
    qkv,
    prob,
    w_out,
    d_res_out,
    d_qkv_out,
    send,
    keep,
    normed_ref,
    ctx_ref,
    d_ctx_ref,
    d_res_ref,
    d_qkv_ref,
    left_qkv,
    left_out,
    factor,
):
    place = [place_ref[i] for i in range(5)]
    d_res_out[...] = interleave(d_last[...].astype(F32), d_tail[...].astype(F32)).astype(BF)
    windows_back(d_res_out, qkv, prob, d_ctx_ref, d_qkv_ref, w_out, 288)
    d_qkv_out[...] = d_qkv_ref[288:576]
    for half, (x, ctx, d_res) in enumerate(
        ((x_first, ctx_first, d_first), (x_second, ctx_second, d_res_out))
    ):
        rows = slice(half * 288, (half + 1) * 288)
        (normed,), _ = norm_parts([x[...].astype(F32)])
        normed_ref[rows] = normed.astype(BF)
        ctx_ref[rows] = ctx[...]
        d_res_ref[rows] = d_res[...]
    d_qkv_ref[0:288] = d_qkv_first[...]
    choice = row_choice(place, 128, 128, 4, True)
    for y in range(4):
        lanes = span((place[0] + y) & 3, 128)
        block = dot_nt(choice, normed_ref[:, lanes]).astype(BF)
        other = dot_nt(choice, ctx_ref[:, lanes]).astype(BF)
        for cz in range(8):
            rows = slice((cz * 4 + y) * 16, (cz * 4 + y + 1) * 16)
            left_qkv[rows] = block[cz * 16 : (cz + 1) * 16]
            left_out[rows] = other[cz * 16 : (cz + 1) * 16]
    for n in range(4):
        columns = slice(n * 512, (n + 1) * 512)
        if n < 3:
            part = dot(left_qkv[...], d_qkv_ref[:, columns])
        else:
            part = dot(left_out[...], d_res_ref[...])
        part = (part * factor).astype(BF)
        keep[:, columns] = part[:256]
        send[:, columns] = part[256:]


def last_back_kernel(d_res, d_qkv, x, w_qkv, d_last, d_tail):
    d_input = input_back(d_res, d_qkv, x, w_qkv)
    d_last[...] = first_rows(d_input).astype(BF)
    d_tail[...] = last_rows(d_input).astype(BF)


def place_result_kernel(body, last, tail, put_body, put_last, put_tail, out, placed):
    placed[...] = jnp.zeros_like(placed)
    out[...] = (
        dot(put_body[...], body[...]) + dot(put_last[...], last[...]) + dot(put_tail[...], tail[...])
    ).astype(BF)


def call(kernel, outs, scratch=(), scalars=0, far=(), far_outs=(), us=1, room=4, after=(), limit=None, through=()):
    def run(*args):
        in_specs = [
            pl.BlockSpec(
                memory_space=pltpu.SMEM if i < scalars else pltpu.HBM if i in far else pltpu.VMEM
            )
            for i in range(len(args))
        ]
        out_specs = [
            pl.BlockSpec(memory_space=pltpu.HBM if i in far_outs else pltpu.VMEM)
            for i in range(len(outs))
        ]
        held = sum(a.size * a.dtype.itemsize for i, a in enumerate(args) if i not in far)
        shapes = [o for i, o in enumerate(outs) if i not in far_outs] + list(scratch)
        held += sum(int(np.prod(s)) * jnp.dtype(d).itemsize for s, d in shapes)
        scratch_shapes = [pltpu.VMEM(shape, dtype) for shape, dtype in scratch]
        for moved in (far, far_outs):
            if moved:
                scratch_shapes.append(pltpu.SemaphoreType.DMA((len(moved),)))
        body = kernel
        idle = len(through) + len(after)
        if idle:

            def body(*refs):
                refs = refs[: len(args)] + refs[len(args) + idle :]
                results = len(args) + len(outs)
                kernel(*refs[:results], *refs[results + len(through) :])

        return pl.pallas_call(
            body,
            out_shape=[jax.ShapeDtypeStruct(shape, dtype) for shape, dtype in outs]
            + [jax.ShapeDtypeStruct(a.shape, a.dtype) for a in through],
            in_specs=in_specs + [pl.BlockSpec(memory_space=pl.ANY)] * idle,
            out_specs=out_specs + [pl.BlockSpec(memory_space=pl.ANY)] * len(through),
            input_output_aliases={len(args) + i: len(outs) + i for i in range(len(through))},
            scratch_shapes=scratch_shapes,
            cost_estimate=pl.CostEstimate(
                flops=int(us * 1e9), bytes_accessed=int(us * 3e6), transcendentals=0
            ),
            compiler_params=pltpu.CompilerParams(
                vmem_limit_bytes=limit * MIB if limit else int(held * 1.15) + room * MIB
            ),
        )(*args, *through, *after)

    return run


def route(move):
    pairs = []
    for source in range(128):
        lon, lat = divmod(source, 8)
        y, x_lo, core, z, x_hi = move(lon >> 2, (lon >> 1) & 1, lon & 1, lat >> 1, lat & 1)
        pairs.append((source, (((y & 3) * 2 + x_lo) * 2 + core) * 8 + (z & 3) * 2 + x_hi))
    return pairs


def groups():
    return [
        [((y * 2 + x_lo) * 2 + core) * 8 + z * 2 + x_hi for y in range(4) for x_lo in range(2) for x_hi in range(2)]
        for core in range(2)
        for z in range(4)
    ]


def send_core(x):
    return lax.ppermute(x, ("lon", "lat"), route(lambda y, xl, c, z, xh: (y, xl, 1 - c, z, xh)))


def send_z(x, d):
    return lax.ppermute(x, ("lon", "lat"), route(lambda y, xl, c, z, xh: (y, xl, c, z + d, xh)))


def send_y(x, d):
    return lax.ppermute(x, ("lon", "lat"), route(lambda y, xl, c, z, xh: (y + d, xl, c, z, xh)))


def send_x_lo(x):
    return lax.ppermute(x, ("lon", "lat"), route(lambda y, xl, c, z, xh: (y, 1 - xl, c, z, xh)))


def send_lon(x, step, partner):
    pairs = []
    for lon in range(16):
        for lat in range(8):
            pairs.append((lon * 8 + lat, (lon + step) % 16 * 8 + (lat ^ partner)))
    return lax.ppermute(x, ("lon", "lat"), pairs)


def add(*refs):
    return sum(r.astype(F32) for r in refs)


def wide_split_kernel(keep_a, got_a, keep_m, got_m, *pieces):
    def by_z(d, o):
        return (
            add(keep_a[d, o, :, :2048], got_a[d, o, :, :2048]).astype(BF),
            add(keep_m[d, o, :, :1024], got_m[d, o, :, :1024]).astype(BF),
        )

    def by_y(d, o):
        return (
            add(keep_a[o, d, :, 2048:], got_a[o, d, :, 2048:]).astype(BF),
            add(keep_m[o, d, :, 1024:], got_m[o, d, :, 1024:]).astype(BF),
        )

    for ring, block in ((pieces[:5], by_z), (pieces[5:], by_y)):
        for d, ref in ((0, ring[0]), (1, ring[1]), (3, ring[2])):
            for o in range(4):
                ref[o, :, :2048], ref[o, :, 2048:] = block(d, o)
        for o in range(4):
            ref = ring[3 + o // 2]
            ref[o % 2, :, :2048], ref[o % 2, :, 2048:] = block(2, o)


def wide_pass_kernel(*refs):
    for ring in range(2):
        up, down, from_below, from_above, up_out, down_out = refs[ring * 4 : ring * 4 + 4] + refs[8 + ring * 2 : 10 + ring * 2]
        for o in range(4):
            if o < 2:
                up_out[o] = add(up[o], from_below[o]).astype(BF)
                down_out[o] = down[o]
            else:
                up_out[o] = up[o]
                down_out[o] = add(down[o], from_above[o - 2]).astype(BF)


def wide_sum_kernel(*refs):
    first, last, by_y, by_z = refs[:3], refs[3:6], refs[6:10], refs[10]
    for d in range(4):
        by_y[d][...] = add(*(r[d] for r in first)).astype(BF)
        by_z[d] = add(*(r[d] for r in last)).astype(BF)


def joint_split_kernel(last, keep, got, *to_z):
    for d in range(4):
        for y in range(4):
            to_z[d][:, y * 2048 : (y + 1) * 2048] = add(keep[d, y], got[d, y]).astype(BF)
        to_z[d][:, 8192:] = last[d]


def joint_sum_kernel(place_ref, *refs):
    from_z, from_y, fine, wide_keep, wide_send = refs[:4], refs[4:8], refs[8], refs[9], refs[10]
    for d in range(4):
        y = (place_ref[0] + d) & 3
        sums = add(*(r[:, d * 2048 : (d + 1) * 2048] for r in from_z))
        for x_lo in range(2):
            for x_hi in range(2):
                device = y * 4 + (place_ref[1] ^ x_lo) * 2 + (place_ref[4] ^ x_hi)
                row = x_lo * 8 + x_hi * 4
                fine[device] = sums[row : row + 4].astype(BF)
    first = add(*(r[...] for r in from_y))
    last = add(*(r[:, 8192:] for r in from_z))
    for wide, rows in ((wide_keep, slice(0, 8)), (wide_send, slice(8, 16))):
        wide[:, :3072] = first[rows].astype(BF)
        wide[:, 3072:] = last[rows].astype(BF)


def shares_kernel(fine_got, wide_keep, wide_got, fine_qkv, fine_out, merge, coarse_qkv, coarse_out):
    fine = add(*(fine_got[d] for d in range(16)))
    fine_qkv[...] = fine[:, :1536]
    fine_out[...] = fine[:, 1536:]
    wide = add(wide_keep[...], wide_got[...])
    coarse_qkv[:, :2048] = wide[:, :2048]
    coarse_qkv[:, 2048:] = wide[:, 3072:4096]
    coarse_out[...] = wide[:, 4096:5120]
    merge[0:8] = wide[:, 2048:3072]
    merge[8:16] = wide[:, 5120:6144]


def blocks(x):
    return x.reshape(4, 4, 16, x.shape[1])


def local(tokens, cotangent, fine_qkv, fine_out, merge_weight, coarse_qkv, coarse_out):
    factor = (144 * lax.axis_size("lon") * lax.axis_size("lat")) ** (-0.5)
    place = axis_places()
    put_own, put_halo = (jnp.asarray(a, BF) for a in place_tokens())
    stack = place_stacked()
    unstack = [jnp.asarray(a.T, BF) for a in stack]
    stack = [jnp.asarray(a, BF) for a in stack]
    result = [jnp.asarray(a, BF) for a in place_result()]

    tok = tokens.transpose(0, 2, 1, 3)
    halo = send_lon(tok[:, :, :8], -1, 0).reshape(192, 512)
    cot_own = cotangent.reshape(144, 1024)
    cot_far = send_lon(cot_own, 0, 1)

    stash = [((288, 512), BF), ((288, 1536), BF), ((288, 512), BF), ((8, 144, 288), BF)]
    fine_weights = [((512, 1536), BF), ((512, 512), BF)]
    body, x_last, x_first, qkv_first, ctx_first, prob_first = call(
        first_forward_kernel,
        [((288, 512), BF), ((144, 512), BF)] + stash,
        stash + [((576, 512), BF), ((432, 576), BF)] + fine_weights,
        far=(0, 1, 2, 3),
        far_outs=(2, 3, 4, 5),
        us=6,
        limit=60,
    )(tok.reshape(576, 512), put_own, fine_qkv, fine_out)
    body_far = send_lon(body, 0, 1)
    last, tail, x_second, qkv_second, ctx_second, prob_second = call(
        second_forward_kernel,
        [((144, 512), BF)] * 2 + stash,
        stash + [((144, 512), BF), ((192, 512), BF), ((144, 192), BF)] + fine_weights,
        far=(0, 1, 2, 3, 4),
        far_outs=(2, 3, 4, 5),
        us=0.01,
        limit=60,
    )(x_last, halo, put_halo, fine_qkv, fine_out)
    tail_own = send_lon(tail, 1, 0)
    tail_far = send_lon(tail, 1, 1)
    last_far = send_lon(last, 0, 1)
    cot, d_ctx = call(cotangent_kernel, [((288, 1024), BF)] * 2, us=3)(cot_own, cot_far, coarse_out)

    merged, ctx, d_qkv, stacked, send_a, keep_a = call(
        functools.partial(coarse_kernel, factor=factor),
        [
            ((288, 1024), BF),
            ((288, 1024), BF),
            ((288, 3072), BF),
            ((4, 288, 512), BF),
            ((256, 4096), BF),
            ((256, 4096), BF),
        ],
        [
            ((288, 1024), BF),
            ((288, 3072), BF),
            ((512, 288), BF),
            ((512, 288), BF),
            ((2048, 1024), BF),
            ((1024, 3072), BF),
        ],
        scalars=1,
        far=(12, 13),
        us=20,
        room=8,
    )(
        place,
        body,
        last,
        tail_own,
        body_far,
        last_far,
        tail_far,
        *stack,
        cot,
        d_ctx,
        merge_weight,
        coarse_qkv,
    )
    got_a = send_core(send_a)

    coarse, d_first, d_last, d_tail, send_m, keep_m = call(
        functools.partial(merge_back_kernel, factor=factor),
        [
            ((144, 1024), BF),
            ((288, 512), BF),
            ((144, 512), BF),
            ((144, 512), BF),
            ((256, 2048), BF),
            ((256, 2048), BF),
        ],
        [
            ((4, 288, 512), BF),
            ((288, 1024), BF),
            ((576, 512), BF),
            ((2, 512, 288), BF),
        ],
        scalars=1,
        us=12,
        room=8,
    )(place, merged, ctx, d_qkv, stacked, cot, *unstack, coarse_qkv, merge_weight, coarse_out)
    d_tail = send_lon(d_tail, -1, 0)
    got_m = send_core(send_m)

    ring_shapes = ([((4, 16, 3072), BF)] * 3 + [((2, 16, 3072), BF)] * 2) * 2
    pieces = call(wide_split_kernel, ring_shapes, us=4)(
        blocks(keep_a), blocks(got_a), blocks(keep_m), blocks(got_m)
    )
    wide_z, wide_y = pieces[:5], pieces[5:]
    passed = (
        send_z(wide_z[3], 1),
        send_z(wide_z[4], -1),
        send_y(wide_y[3], 1),
        send_y(wide_y[4], -1),
    )

    d_qkv_first, d_x_first = call(
        first_back_kernel,
        [((288, 1536), BF), ((288, 512), BF)],
        [((288, 512), BF)],
        us=8,
        after=(pieces[0],),
    )(d_first, x_first, qkv_first, prob_first, fine_qkv, fine_out)

    up_z, down_z, up_y, down_y = call(
        wide_pass_kernel, [((4, 16, 3072), BF)] * 4, us=2, after=(d_qkv_first,)
    )(wide_z[1], wide_z[2], *passed[:2], wide_y[1], wide_y[2], *passed[2:])
    wide_z = (wide_z[0], send_z(up_z, 1), send_z(down_z, -1))
    wide_y = (wide_y[0], send_y(up_y, 1), send_y(down_y, -1))

    d_res, d_qkv_second, send_f, keep_f = call(
        functools.partial(second_back_kernel, factor=factor),
        [((288, 512), BF), ((288, 1536), BF), ((256, 2048), BF), ((256, 2048), BF)],
        [
            ((576, 512), BF),
            ((576, 512), BF),
            ((288, 512), BF),
            ((576, 512), BF),
            ((576, 1536), BF),
            ((512, 576), BF),
            ((512, 576), BF),
        ],
        scalars=1,
        us=10,
        after=(up_z,),
    )(
        place,
        d_last,
        d_tail,
        d_first,
        d_qkv_first,
        x_first,
        x_second,
        ctx_first,
        ctx_second,
        qkv_second,
        prob_second,
        fine_out,
    )
    *wide_first, wide_last, send_f = call(
        wide_sum_kernel,
        [((16, 3072), BF)] * 4 + [((4, 16, 3072), BF)],
        us=2,
        through=(send_f,),
    )(*wide_z, *wide_y)
    got_f = send_core(send_f)
    d_x_last, d_x_tail = call(last_back_kernel, [((144, 512), BF)] * 2, us=2)(
        d_res, d_qkv_second, x_second, fine_qkv
    )
    d_x_tail = send_lon(d_x_tail, 1, 0)
    to_z = call(joint_split_kernel, [((16, 11264), BF)] * 4, us=1, after=(d_x_last,))(
        wide_last, blocks(keep_f), blocks(got_f)
    )
    from_z = [to_z[0]] + [send_z(to_z[d], d) for d in (1, 2, 3)]
    from_y = [wide_first[0]] + [send_y(wide_first[d], d) for d in (1, 2, 3)]
    d_tokens, placed = call(place_result_kernel, [((576, 512), BF), ((8, 128), F32)], us=2)(
        d_x_first, d_x_last, d_x_tail, *result
    )
    fine, wide_keep, wide_send = call(
        joint_sum_kernel,
        [((16, 4, 2048), BF)] + [((8, 6144), BF)] * 2,
        scalars=1,
        after=(placed,),
    )(place, *from_z, *from_y)
    wide_got = send_x_lo(wide_send)
    fine = lax.all_to_all(fine, ("lon", "lat"), 0, 0, axis_index_groups=groups(), tiled=True)
    shares = call(
        shares_kernel,
        [
            ((4, 1536), F32),
            ((4, 512), F32),
            ((16, 1024), F32),
            ((8, 3072), F32),
            ((8, 1024), F32),
        ],
    )(fine, wide_keep, wide_got)
    return (
        coarse.reshape(4, 12, 3, 1024),
        d_tokens.reshape(4, 6, 24, 512).transpose(0, 2, 1, 3),
        *shares,
    )


def solution(mesh):
    grid_spec = P(None, "lon", "lat", None)
    rows_spec = P(("lon", "lat"), None)
    return jax.shard_map(
        local,
        mesh=mesh,
        in_specs=(grid_spec, grid_spec, P(), P(), P(), P(), P()),
        out_specs=(grid_spec, grid_spec) + (rows_spec,) * 5,
        check_vma=False,
    )
```

```python
import functools

import jax
import jax.numpy as jnp
import numpy as np
from jax import lax
from jax.experimental import pallas as pl
from jax.experimental.pallas import tpu as pltpu
from jax.sharding import PartitionSpec as P

HEADS = 8
HEADS2 = 16
NORM_EPS = 1e-05
BF = jnp.bfloat16
F32 = jnp.float32
VMEM = pl.BlockSpec(memory_space=pltpu.VMEM)
MIB = 1024 * 1024


def place_tokens():
    own = np.zeros((432, 576), np.float32)
    halo = np.zeros((144, 192), np.float32)
    for pair in range(2):
        for quarter in range(4):
            for level in range(2):
                for lat in range(6):
                    for lon in range(6):
                        inner = level * 36 + lat * 6 + lon
                        line = (2 * pair + level) * 6 + lat
                        if quarter < 2:
                            own[pair * 144 + quarter * 72 + inner, line * 24 + 6 * quarter + lon + 6] = 1
                        elif quarter == 2:
                            own[288 + pair * 72 + inner, line * 24 + lon + 18] = 1
                        else:
                            halo[pair * 72 + inner, line * 8 + lon] = 1
    return own, halo


def place_stacked():
    body = np.zeros((576, 288), np.float32)
    last = np.zeros((576, 144), np.float32)
    tail = np.zeros((576, 144), np.float32)
    for a in range(2):
        for b in range(2):
            for pair in range(2):
                for level in range(2):
                    for i in range(12):
                        for j in range(3):
                            row = (a * 2 + b) * 144 + pair * 72 + level * 36 + i * 3 + j
                            quarter, lon, lat = i // 3, 2 * (i % 3) + a, 2 * j + b
                            inner = level * 36 + lat * 6 + lon
                            if quarter == 0:
                                tail[row, pair * 72 + inner] = 1
                            elif quarter == 3:
                                last[row, pair * 72 + inner] = 1
                            else:
                                body[row, pair * 144 + (quarter - 1) * 72 + inner] = 1
    return body, last, tail


def place_result():
    body = np.zeros((576, 288), np.float32)
    last = np.zeros((576, 144), np.float32)
    tail = np.zeros((576, 144), np.float32)
    for level in range(4):
        for lat in range(6):
            for lon in range(24):
                row = (level * 6 + lat) * 24 + lon
                inner = (level % 2) * 36 + lat * 6 + lon % 6
                if lon < 6:
                    tail[row, (level // 2) * 72 + inner] = 1
                elif lon >= 18:
                    last[row, (level // 2) * 72 + inner] = 1
                else:
                    body[row, (level // 2) * 144 + (lon // 6 - 1) * 72 + inner] = 1
    return body, last, tail


def dot(a, b):
    return lax.dot_general(a, b, (((1,), (0,)), ((), ())), preferred_element_type=F32)


def dot_nt(a, b):
    return lax.dot_general(a, b, (((1,), (1,)), ((), ())), preferred_element_type=F32)


def dot_tn(a, b):
    return lax.dot_general(a, b, (((0,), (0,)), ((), ())), preferred_element_type=F32)


def steps(count, body):
    lax.fori_loop(0, count, lambda i, carry: (body(i), carry)[1], 0)


def span(i, size):
    return pl.ds(pl.multiple_of(i * size, size), size)


def total(x):
    return jnp.sum(x, axis=-1, keepdims=True)


def norm_parts(parts):
    width = sum(p.shape[1] for p in parts)
    mean = sum(total(p) for p in parts) * (1.0 / width)
    centred = [p - mean for p in parts]
    rstd = lax.rsqrt(sum(total(c * c) for c in centred) * (1.0 / width) + NORM_EPS)
    return [c * rstd for c in centred], rstd


def norm_back(normed, rstd, upstream):
    width = sum(p.shape[1] for p in normed)
    first = sum(total(u) for u in upstream) * (1.0 / width)
    second = sum(total(u * n) for u, n in zip(upstream, normed)) * (1.0 / width)
    return [rstd * (u - first - n * second) for u, n in zip(upstream, normed)]


def half_masks(rows):
    lane = lax.broadcasted_iota(jnp.int32, (rows, 128), 1)
    low = lane < 64
    return low, jnp.where(low, 1.0, 0.0).astype(BF), jnp.where(low, 0.0, 1.0).astype(BF)


def two_heads(x, masks):
    return jnp.concatenate([x * masks[1], x * masks[2]], axis=0)


def one_row(x, masks):
    rows = x.shape[0] // 2
    return jnp.where(masks[0], x[:rows], x[rows:])


def softmax(scores):
    shifted = jnp.exp(scores - jnp.max(scores, axis=0, keepdims=True))
    return shifted * (1.0 / jnp.sum(shifted, axis=0, keepdims=True))


def attend_back(queries, keys, values, d_context, probs, weights, masks):
    d_weights = dot_nt(values, d_context)
    mean = jnp.sum(d_weights * probs, axis=0, keepdims=True)
    d_scores = (probs * (d_weights - mean)).astype(BF)
    d_queries = one_row(dot_tn(d_scores, keys), masks)
    return d_queries, dot(d_scores, queries), dot(weights, d_context)


def axis_places():
    lon, lat = lax.axis_index("lon"), lax.axis_index("lat")
    return jnp.stack([lon >> 2, (lon >> 1) & 1, lon & 1, lat >> 1, lat & 1]).astype(jnp.int32)


def row_choice(place, rows, features, per_share, both_halves):
    r = lax.broadcasted_iota(jnp.int32, (rows, features), 0)
    col = lax.broadcasted_iota(jnp.int32, (rows, features), 1)
    low = r & (per_share - 1)
    r = r >> (per_share.bit_length() - 1)
    if both_halves:
        x_hi = (r & 1) ^ place[4]
        r = r >> 1
    else:
        x_hi = place[4]
    x_lo = (r & 1) ^ place[1]
    z = ((r >> 1) + place[3]) & 3
    core = ((r >> 3) & 1) ^ place[2]
    share = ((x_lo * 2 + core) * 8) + z * 2 + x_hi
    return jnp.where(share * per_share + low == col, 1.0, 0.0).astype(BF)


def interleave(own, far):
    return jnp.concatenate([own[:72], far[:72], own[72:], far[72:]], axis=0)


def first_rows(x):
    return jnp.concatenate([x[0:72], x[144:216]], axis=0)


def last_rows(x):
    return jnp.concatenate([x[72:144], x[216:288]], axis=0)


def fetch(sems, *pairs):
    copies = [pltpu.make_async_copy(src, dst, sems.at[i]) for i, (src, dst) in enumerate(pairs)]
    for copy in copies:
        copy.start()
    return copies


def window_forward(x, w_qkv, w_out, loads, stash, stash_out, sems):
    stores = [pltpu.make_async_copy(a, b, sems.at[i]) for i, (a, b) in enumerate(zip(stash, stash_out))]
    x_ref, qkv, ctx, prob = stash
    x_ref[...] = x.astype(BF)
    stores[0].start()
    (normed,), _ = norm_parts([x])
    normed = normed.astype(BF)
    if loads:
        loads[0].wait()
    for n in range(3):
        part = dot(normed, w_qkv[:, n * 512 : (n + 1) * 512])
        if n == 0:
            part = part * (512 // HEADS) ** (-0.5)
        qkv[:, n * 512 : (n + 1) * 512] = part.astype(BF)
    stores[1].start()
    masks = half_masks(144)
    for w in range(2):
        rows = slice(w * 144, (w + 1) * 144)
        for h in range(4):
            lanes = slice(h * 128, (h + 1) * 128)
            queries = two_heads(qkv[rows, lanes], masks)
            keys = qkv[rows, 512 + h * 128 : 512 + (h + 1) * 128]
            values = qkv[rows, 1024 + h * 128 : 1024 + (h + 1) * 128]
            weights = softmax(dot_nt(keys, queries)).astype(BF)
            prob[w * 4 + h] = weights
            ctx[rows, lanes] = one_row(dot_tn(weights, values), masks).astype(BF)
    stores[3].start()
    stores[2].start()
    if loads:
        loads[1].wait()
    return x + dot(ctx[...], w_out[...]), stores


def first_forward_kernel(
    tok_in, put_in, w_qkv_in, w_out_in, result, x_last, *refs
):
    stash_out, stash, (tok, put, w_qkv, w_out, sems, out_sems) = refs[:4], refs[4:8], refs[8:]
    loads = fetch(sems, (tok_in, tok), (put_in, put), (w_qkv_in, w_qkv), (w_out_in, w_out))
    loads[0].wait()
    loads[1].wait()
    x = dot(put[...], tok[...])
    x_last[...] = x[288:].astype(BF)
    y, stores = window_forward(x[:288], w_qkv, w_out, loads[2:], stash, stash_out, out_sems)
    result[...] = y.astype(BF)
    for store in stores:
        store.wait()


def second_forward_kernel(
    x_last_in, halo, put_halo_in, w_qkv_in, w_out_in, last, tail, *refs
):
    stash_out, stash, (x_last, put_halo, w_qkv, w_out, sems, out_sems) = (
        refs[:4],
        refs[4:8],
        refs[8:],
    )
    loads = fetch(
        sems,
        (x_last_in, x_last),
        (put_halo_in, put_halo),
        (w_qkv_in, w_qkv),
        (w_out_in, w_out),
    )
    for load in loads[:2]:
        load.wait()
    x = interleave(x_last[...].astype(F32), dot(put_halo[...], halo[...]))
    y, stores = window_forward(x, w_qkv, w_out, loads[2:], stash, stash_out, out_sems)
    last[...] = first_rows(y).astype(BF)
    tail[...] = last_rows(y).astype(BF)
    for store in stores:
        store.wait()


def cotangent_kernel(cot_own, cot_far, w_out, cot, d_ctx):
    cot[...] = interleave(cot_own[...].astype(F32), cot_far[...].astype(F32)).astype(BF)
    for n in range(2):
        lanes = slice(n * 512, (n + 1) * 512)
        d_ctx[:, lanes] = dot_nt(cot[...], w_out[lanes, :]).astype(BF)


def coarse_kernel(
    place_ref,
    body_own,
    last_own,
    tail_own,
    body_far,
    last_far,
    tail_far,
    put_body,
    put_last,
    put_tail,
    cot,
    d_ctx,
    w_merge_in,
    w_qkv_in,
    merged_ref,
    ctx_ref,
    d_qkv_ref,
    stacked_out,
    send,
    keep,
    normed_ref,
    qkv_ref,
    left_qkv,
    left_out,
    w_merge,
    w_qkv,
    sems,
    factor,
):
    loads = fetch(sems, (w_merge_in, w_merge), (w_qkv_in, w_qkv))
    place = [place_ref[i] for i in range(5)]

    def stack(body, last, tail):
        return (
            dot(put_body[...], body[...])
            + dot(put_last[...], last[...])
            + dot(put_tail[...], tail[...])
        )

    own = stack(body_own, last_own, tail_own)
    far = stack(body_far, last_far, tail_far)
    parts = [interleave(own[g * 144 : (g + 1) * 144], far[g * 144 : (g + 1) * 144]) for g in range(4)]
    for g in range(4):
        stacked_out[g] = parts[g].astype(BF)
    normed, _ = norm_parts(parts)
    loads[0].wait()
    merged = sum(dot(normed[g].astype(BF), w_merge[g * 512 : (g + 1) * 512, :]) for g in range(4))
    merged_ref[...] = merged.astype(BF)
    merged = merged_ref[...].astype(F32)
    (normed,), _ = norm_parts([merged])
    normed_ref[...] = normed.astype(BF)
    loads[1].wait()

    def project(n):
        part = dot(normed_ref[...], w_qkv[:, span(n, 512)])
        scale = jnp.where(n < 2, (1024 // HEADS2) ** (-0.5), 1.0)
        qkv_ref[:, span(n, 512)] = (part * scale).astype(BF)

    steps(6, project)
    masks = half_masks(144)
    for h in range(8):
        lanes, key_lanes, value_lanes = (slice(n * 128, (n + 1) * 128) for n in (h, h + 8, h + 16))
        for pair in range(2):
            rows = slice(pair * 144, (pair + 1) * 144)
            queries = two_heads(qkv_ref[rows, lanes], masks)
            keys = qkv_ref[rows, key_lanes]
            values = qkv_ref[rows, value_lanes]
            d_context = two_heads(d_ctx[rows, lanes], masks)
            probs = softmax(dot_nt(keys, queries))
            weights = probs.astype(BF)
            ctx_ref[rows, lanes] = one_row(dot_tn(weights, values), masks).astype(BF)
            d_queries, d_keys, d_values = attend_back(
                queries, keys, values, d_context, probs, weights, masks
            )
            d_qkv_ref[rows, lanes] = (d_queries * (1024 // HEADS2) ** (-0.5)).astype(BF)
            d_qkv_ref[rows, key_lanes] = d_keys.astype(BF)
            d_qkv_ref[rows, value_lanes] = d_values.astype(BF)

    choice = row_choice(place, 128, 256, 8, False)
    for y in range(4):
        lanes = span((place[0] + y) & 3, 256)
        block = dot_nt(choice, normed_ref[:, lanes]).astype(BF)
        other = dot_nt(choice, ctx_ref[:, lanes]).astype(BF)
        for cz in range(8):
            rows = slice((cz * 4 + y) * 16, (cz * 4 + y + 1) * 16)
            left_qkv[rows] = block[cz * 16 : (cz + 1) * 16]
            left_out[rows] = other[cz * 16 : (cz + 1) * 16]

    def grads_qkv(n):
        part = (dot(left_qkv[...], d_qkv_ref[:, span(n, 512)]) * factor).astype(BF)
        keep[:, span(n, 512)] = part[:256]
        send[:, span(n, 512)] = part[256:]

    steps(6, grads_qkv)

    def grads_out(n):
        part = (dot(left_out[...], cot[:, span(n, 512)]) * factor).astype(BF)
        keep[:, span(n + 6, 512)] = part[:256]
        send[:, span(n + 6, 512)] = part[256:]

    steps(2, grads_out)


def merge_back_kernel(
    place_ref,
    merged,
    ctx,
    d_qkv,
    stacked,
    cot,
    put_body,
    put_last,
    put_tail,
    w_qkv,
    w_merge,
    w_out,
    coarse,
    d_body,
    d_last,
    d_tail,
    send,
    keep,
    normed_ref,
    d_merged_ref,
    d_stacked_ref,
    left,
    factor,
):
    place = [place_ref[i] for i in range(5)]
    stack_normed, stack_rstd = norm_parts([stacked[g].astype(F32) for g in range(4)])
    for g in range(4):
        normed_ref[g] = stack_normed[g].astype(BF)
    d_normed = jnp.zeros((288, 1024), F32)
    for n in range(3):
        d_normed = d_normed + dot_nt(
            d_qkv[:, n * 1024 : (n + 1) * 1024], w_qkv[:, n * 1024 : (n + 1) * 1024]
        )
    d_normed = d_normed.astype(BF).astype(F32)
    (normed,), rstd = norm_parts([merged[...].astype(F32)])
    (d_input,) = norm_back([normed], rstd, [d_normed])
    d_input = cot[...].astype(F32) + d_input
    d_merged_ref[...] = d_input.astype(BF)
    d_own = first_rows(d_input).astype(BF)

    upstream = []
    for g in range(4):
        part = dot_nt(d_own, w_merge[g * 512 : (g + 1) * 512, :])
        upstream.append(part.astype(BF).astype(F32))
    own = norm_back([first_rows(n) for n in stack_normed], first_rows(stack_rstd), upstream)
    for g in range(4):
        d_stacked_ref[g * 144 : (g + 1) * 144, :] = own[g].astype(BF)
    d_tail[...] = dot(put_tail[...], d_stacked_ref[...]).astype(BF)
    d_body[...] = dot(put_body[...], d_stacked_ref[...]).astype(BF)
    d_last[...] = dot(put_last[...], d_stacked_ref[...]).astype(BF)

    choice = row_choice(place, 256, 512, 16, False)
    for y in range(4):
        block = dot_nt(choice, normed_ref[(place[0] + y) & 3])
        for cz in range(8):
            for half in range(2):
                start = cz * 32 + half * 8
                rows = jnp.concatenate([block[start : start + 8], block[start + 16 : start + 24]], axis=0)
                left[half, (cz * 4 + y) * 16 : (cz * 4 + y + 1) * 16] = rows.astype(BF)
    for n in range(4):
        columns = slice(n * 512, (n + 1) * 512)
        part = dot(left[n // 2], d_merged_ref[:, (n % 2) * 512 : (n % 2 + 1) * 512])
        part = (part * factor).astype(BF)
        keep[:, columns] = part[:256]
        send[:, columns] = part[256:]

    projected = dot(ctx[...], w_out[...])
    coarse[...] = first_rows(merged[...].astype(F32) + projected).astype(BF)


def windows_back(d_res, qkv, prob, d_ctx_ref, d_qkv_ref, w_out, first):
    d_ctx_ref[...] = dot_nt(d_res[...], w_out[...]).astype(BF)
    masks = half_masks(144)
    for w in range(2):
        rows = slice(w * 144, (w + 1) * 144)
        put = slice(first + w * 144, first + (w + 1) * 144)
        for h in range(4):
            lanes = slice(h * 128, (h + 1) * 128)
            key_lanes = slice(512 + h * 128, 512 + (h + 1) * 128)
            value_lanes = slice(1024 + h * 128, 1024 + (h + 1) * 128)
            weights = prob[w * 4 + h]
            d_queries, d_keys, d_values = attend_back(
                two_heads(qkv[rows, lanes], masks),
                qkv[rows, key_lanes],
                qkv[rows, value_lanes],
                two_heads(d_ctx_ref[rows, lanes], masks),
                weights.astype(F32),
                weights,
                masks,
            )
            d_qkv_ref[put, lanes] = (d_queries * (512 // HEADS) ** (-0.5)).astype(BF)
            d_qkv_ref[put, key_lanes] = d_keys.astype(BF)
            d_qkv_ref[put, value_lanes] = d_values.astype(BF)


def input_back(d_res, d_qkv, x, w_qkv):
    (normed,), rstd = norm_parts([x[...].astype(F32)])
    d_normed = dot_nt(d_qkv[...], w_qkv[...]).astype(BF).astype(F32)
    (d_input,) = norm_back([normed], rstd, [d_normed])
    return d_res[...].astype(F32) + d_input


def first_back_kernel(d_res, x, qkv, prob, w_qkv, w_out, d_qkv, d_x, d_ctx_ref):
    windows_back(d_res, qkv, prob, d_ctx_ref, d_qkv, w_out, 0)
    d_x[...] = input_back(d_res, d_qkv, x, w_qkv).astype(BF)


def second_back_kernel(
    place_ref,
    d_last,
    d_tail,
    d_first,
    d_qkv_first,
    x_first,
    x_second,
    ctx_first,
    ctx_second,
    qkv,
    prob,
    w_out,
    d_res_out,
    d_qkv_out,
    send,
    keep,
    normed_ref,
    ctx_ref,
    d_ctx_ref,
    d_res_ref,
    d_qkv_ref,
    left_qkv,
    left_out,
    factor,
):
    place = [place_ref[i] for i in range(5)]
    d_res_out[...] = interleave(d_last[...].astype(F32), d_tail[...].astype(F32)).astype(BF)
    windows_back(d_res_out, qkv, prob, d_ctx_ref, d_qkv_ref, w_out, 288)
    d_qkv_out[...] = d_qkv_ref[288:576]
    for half, (x, ctx, d_res) in enumerate(
        ((x_first, ctx_first, d_first), (x_second, ctx_second, d_res_out))
    ):
        rows = slice(half * 288, (half + 1) * 288)
        (normed,), _ = norm_parts([x[...].astype(F32)])
        normed_ref[rows] = normed.astype(BF)
        ctx_ref[rows] = ctx[...]
        d_res_ref[rows] = d_res[...]
    d_qkv_ref[0:288] = d_qkv_first[...]
    choice = row_choice(place, 128, 128, 4, True)
    for y in range(4):
        lanes = span((place[0] + y) & 3, 128)
        block = dot_nt(choice, normed_ref[:, lanes]).astype(BF)
        other = dot_nt(choice, ctx_ref[:, lanes]).astype(BF)
        for cz in range(8):
            rows = slice((cz * 4 + y) * 16, (cz * 4 + y + 1) * 16)
            left_qkv[rows] = block[cz * 16 : (cz + 1) * 16]
            left_out[rows] = other[cz * 16 : (cz + 1) * 16]
    for n in range(4):
        columns = slice(n * 512, (n + 1) * 512)
        if n < 3:
            part = dot(left_qkv[...], d_qkv_ref[:, columns])
        else:
            part = dot(left_out[...], d_res_ref[...])
        part = (part * factor).astype(BF)
        keep[:, columns] = part[:256]
        send[:, columns] = part[256:]


def last_back_kernel(d_res, d_qkv, x, w_qkv, d_last, d_tail):
    d_input = input_back(d_res, d_qkv, x, w_qkv)
    d_last[...] = first_rows(d_input).astype(BF)
    d_tail[...] = last_rows(d_input).astype(BF)


def place_result_kernel(body, last, tail, put_body, put_last, put_tail, out, placed):
    placed[...] = jnp.zeros_like(placed)
    out[...] = (
        dot(put_body[...], body[...]) + dot(put_last[...], last[...]) + dot(put_tail[...], tail[...])
    ).astype(BF)


def call(kernel, outs, scratch=(), scalars=0, far=(), far_outs=(), us=1, room=4, after=(), limit=None, through=()):
    def run(*args):
        in_specs = [
            pl.BlockSpec(
                memory_space=pltpu.SMEM if i < scalars else pltpu.HBM if i in far else pltpu.VMEM
            )
            for i in range(len(args))
        ]
        out_specs = [
            pl.BlockSpec(memory_space=pltpu.HBM if i in far_outs else pltpu.VMEM)
            for i in range(len(outs))
        ]
        held = sum(a.size * a.dtype.itemsize for i, a in enumerate(args) if i not in far)
        shapes = [o for i, o in enumerate(outs) if i not in far_outs] + list(scratch)
        held += sum(int(np.prod(s)) * jnp.dtype(d).itemsize for s, d in shapes)
        scratch_shapes = [pltpu.VMEM(shape, dtype) for shape, dtype in scratch]
        for moved in (far, far_outs):
            if moved:
                scratch_shapes.append(pltpu.SemaphoreType.DMA((len(moved),)))
        body = kernel
        idle = len(through) + len(after)
        if idle:

            def body(*refs):
                refs = refs[: len(args)] + refs[len(args) + idle :]
                results = len(args) + len(outs)
                kernel(*refs[:results], *refs[results + len(through) :])

        return pl.pallas_call(
            body,
            out_shape=[jax.ShapeDtypeStruct(shape, dtype) for shape, dtype in outs]
            + [jax.ShapeDtypeStruct(a.shape, a.dtype) for a in through],
            in_specs=in_specs + [pl.BlockSpec(memory_space=pl.ANY)] * idle,
            out_specs=out_specs + [pl.BlockSpec(memory_space=pl.ANY)] * len(through),
            input_output_aliases={len(args) + i: len(outs) + i for i in range(len(through))},
            scratch_shapes=scratch_shapes,
            cost_estimate=pl.CostEstimate(
                flops=int(us * 1e9), bytes_accessed=int(us * 3e6), transcendentals=0
            ),
            compiler_params=pltpu.CompilerParams(
                vmem_limit_bytes=limit * MIB if limit else int(held * 1.15) + room * MIB
            ),
        )(*args, *through, *after)

    return run


def route(move):
    pairs = []
    for source in range(128):
        lon, lat = divmod(source, 8)
        y, x_lo, core, z, x_hi = move(lon >> 2, (lon >> 1) & 1, lon & 1, lat >> 1, lat & 1)
        pairs.append((source, (((y & 3) * 2 + x_lo) * 2 + core) * 8 + (z & 3) * 2 + x_hi))
    return pairs


def groups():
    return [
        [((y * 2 + x_lo) * 2 + core) * 8 + z * 2 + x_hi for y in range(4) for x_lo in range(2) for x_hi in range(2)]
        for core in range(2)
        for z in range(4)
    ]


def send_core(x):
    return lax.ppermute(x, ("lon", "lat"), route(lambda y, xl, c, z, xh: (y, xl, 1 - c, z, xh)))


def send_z(x, d):
    return lax.ppermute(x, ("lon", "lat"), route(lambda y, xl, c, z, xh: (y, xl, c, z + d, xh)))


def send_y(x, d):
    return lax.ppermute(x, ("lon", "lat"), route(lambda y, xl, c, z, xh: (y + d, xl, c, z, xh)))


def send_x_lo(x):
    return lax.ppermute(x, ("lon", "lat"), route(lambda y, xl, c, z, xh: (y, 1 - xl, c, z, xh)))


def send_lon(x, step, partner):
    pairs = []
    for lon in range(16):
        for lat in range(8):
            pairs.append((lon * 8 + lat, (lon + step) % 16 * 8 + (lat ^ partner)))
    return lax.ppermute(x, ("lon", "lat"), pairs)


def add(*refs):
    return sum(r.astype(F32) for r in refs)


def wide_split_kernel(keep_a, got_a, keep_m, got_m, *pieces):
    def by_z(d, o):
        return (
            add(keep_a[d, o, :, :2048], got_a[d, o, :, :2048]).astype(BF),
            add(keep_m[d, o, :, :1024], got_m[d, o, :, :1024]).astype(BF),
        )

    def by_y(d, o):
        return (
            add(keep_a[o, d, :, 2048:], got_a[o, d, :, 2048:]).astype(BF),
            add(keep_m[o, d, :, 1024:], got_m[o, d, :, 1024:]).astype(BF),
        )

    for ring, block in ((pieces[:5], by_z), (pieces[5:], by_y)):
        for d, ref in ((0, ring[0]), (1, ring[1]), (3, ring[2])):
            for o in range(4):
                ref[o, :, :2048], ref[o, :, 2048:] = block(d, o)
        for o in range(4):
            ref = ring[3 + o // 2]
            ref[o % 2, :, :2048], ref[o % 2, :, 2048:] = block(2, o)


def wide_pass_kernel(*refs):
    for ring in range(2):
        up, down, from_below, from_above, up_out, down_out = refs[ring * 4 : ring * 4 + 4] + refs[8 + ring * 2 : 10 + ring * 2]
        for o in range(4):
            if o < 2:
                up_out[o] = add(up[o], from_below[o]).astype(BF)
                down_out[o] = down[o]
            else:
                up_out[o] = up[o]
                down_out[o] = add(down[o], from_above[o - 2]).astype(BF)


def wide_sum_kernel(*refs):
    first, last, by_y, by_z = refs[:3], refs[3:6], refs[6:10], refs[10]
    for d in range(4):
        by_y[d][...] = add(*(r[d] for r in first)).astype(BF)
        by_z[d] = add(*(r[d] for r in last)).astype(BF)


def joint_split_kernel(last, keep, got, *to_z):
    for d in range(4):
        for y in range(4):
            to_z[d][:, y * 2048 : (y + 1) * 2048] = add(keep[d, y], got[d, y]).astype(BF)
        to_z[d][:, 8192:] = last[d]


def joint_sum_kernel(place_ref, *refs):
    from_z, from_y, fine, wide_keep, wide_send = refs[:4], refs[4:8], refs[8], refs[9], refs[10]
    for d in range(4):
        y = (place_ref[0] + d) & 3
        sums = add(*(r[:, d * 2048 : (d + 1) * 2048] for r in from_z))
        for x_lo in range(2):
            for x_hi in range(2):
                device = y * 4 + (place_ref[1] ^ x_lo) * 2 + (place_ref[4] ^ x_hi)
                row = x_lo * 8 + x_hi * 4
                fine[device] = sums[row : row + 4].astype(BF)
    first = add(*(r[...] for r in from_y))
    last = add(*(r[:, 8192:] for r in from_z))
    for wide, rows in ((wide_keep, slice(0, 8)), (wide_send, slice(8, 16))):
        wide[:, :3072] = first[rows].astype(BF)
        wide[:, 3072:] = last[rows].astype(BF)


def shares_kernel(fine_got, wide_keep, wide_got, fine_qkv, fine_out, merge, coarse_qkv, coarse_out):
    fine = add(*(fine_got[d] for d in range(16)))
    fine_qkv[...] = fine[:, :1536]
    fine_out[...] = fine[:, 1536:]
    wide = add(wide_keep[...], wide_got[...])
    coarse_qkv[:, :2048] = wide[:, :2048]
    coarse_qkv[:, 2048:] = wide[:, 3072:4096]
    coarse_out[...] = wide[:, 4096:5120]
    merge[0:8] = wide[:, 2048:3072]
    merge[8:16] = wide[:, 5120:6144]


def blocks(x):
    return x.reshape(4, 4, 16, x.shape[1])


def local(tokens, cotangent, fine_qkv, fine_out, merge_weight, coarse_qkv, coarse_out):
    factor = (144 * lax.axis_size("lon") * lax.axis_size("lat")) ** (-0.5)
    place = axis_places()
    put_own, put_halo = (jnp.asarray(a, BF) for a in place_tokens())
    stack = place_stacked()
    unstack = [jnp.asarray(a.T, BF) for a in stack]
    stack = [jnp.asarray(a, BF) for a in stack]
    result = [jnp.asarray(a, BF) for a in place_result()]

    tok = tokens.transpose(0, 2, 1, 3)
    halo = send_lon(tok[:, :, :8], -1, 0).reshape(192, 512)
    cot_own = cotangent.reshape(144, 1024)
    cot_far = send_lon(cot_own, 0, 1)

    stash = [((288, 512), BF), ((288, 1536), BF), ((288, 512), BF), ((8, 144, 288), BF)]
    fine_weights = [((512, 1536), BF), ((512, 512), BF)]
    body, x_last, x_first, qkv_first, ctx_first, prob_first = call(
        first_forward_kernel,
        [((288, 512), BF), ((144, 512), BF)] + stash,
        stash + [((576, 512), BF), ((432, 576), BF)] + fine_weights,
        far=(0, 1, 2, 3),
        far_outs=(2, 3, 4, 5),
        us=6,
        limit=60,
    )(tok.reshape(576, 512), put_own, fine_qkv, fine_out)
    body_far = send_lon(body, 0, 1)
    last, tail, x_second, qkv_second, ctx_second, prob_second = call(
        second_forward_kernel,
        [((144, 512), BF)] * 2 + stash,
        stash + [((144, 512), BF), ((144, 192), BF)] + fine_weights,
        far=(0, 2, 3, 4),
        far_outs=(2, 3, 4, 5),
        us=0.01,
        limit=60,
    )(x_last, halo, put_halo, fine_qkv, fine_out)
    tail_own = send_lon(tail, 1, 0)
    tail_far = send_lon(tail, 1, 1)
    last_far = send_lon(last, 0, 1)
    cot, d_ctx = call(cotangent_kernel, [((288, 1024), BF)] * 2, us=3)(cot_own, cot_far, coarse_out)

    merged, ctx, d_qkv, stacked, send_a, keep_a = call(
        functools.partial(coarse_kernel, factor=factor),
        [
            ((288, 1024), BF),
            ((288, 1024), BF),
            ((288, 3072), BF),
            ((4, 288, 512), BF),
            ((256, 4096), BF),
            ((256, 4096), BF),
        ],
        [
            ((288, 1024), BF),
            ((288, 3072), BF),
            ((512, 288), BF),
            ((512, 288), BF),
            ((2048, 1024), BF),
            ((1024, 3072), BF),
        ],
        scalars=1,
        far=(12, 13),
        us=20,
        room=8,
    )(
        place,
        body,
        last,
        tail_own,
        body_far,
        last_far,
        tail_far,
        *stack,
        cot,
        d_ctx,
        merge_weight,
        coarse_qkv,
    )
    got_a = send_core(send_a)

    coarse, d_first, d_last, d_tail, send_m, keep_m = call(
        functools.partial(merge_back_kernel, factor=factor),
        [
            ((144, 1024), BF),
            ((288, 512), BF),
            ((144, 512), BF),
            ((144, 512), BF),
            ((256, 2048), BF),
            ((256, 2048), BF),
        ],
        [
            ((4, 288, 512), BF),
            ((288, 1024), BF),
            ((576, 512), BF),
            ((2, 512, 288), BF),
        ],
        scalars=1,
        us=12,
        room=8,
    )(place, merged, ctx, d_qkv, stacked, cot, *unstack, coarse_qkv, merge_weight, coarse_out)
    d_tail = send_lon(d_tail, -1, 0)
    got_m = send_core(send_m)

    ring_shapes = ([((4, 16, 3072), BF)] * 3 + [((2, 16, 3072), BF)] * 2) * 2
    pieces = call(wide_split_kernel, ring_shapes, us=4)(
        blocks(keep_a), blocks(got_a), blocks(keep_m), blocks(got_m)
    )
    wide_z, wide_y = pieces[:5], pieces[5:]
    passed = (
        send_z(wide_z[3], 1),
        send_z(wide_z[4], -1),
        send_y(wide_y[3], 1),
        send_y(wide_y[4], -1),
    )

    d_qkv_first, d_x_first = call(
        first_back_kernel,
        [((288, 1536), BF), ((288, 512), BF)],
        [((288, 512), BF)],
        us=8,
        after=(pieces[0],),
    )(d_first, x_first, qkv_first, prob_first, fine_qkv, fine_out)

    up_z, down_z, up_y, down_y = call(
        wide_pass_kernel, [((4, 16, 3072), BF)] * 4, us=2, after=(d_qkv_first,)
    )(wide_z[1], wide_z[2], *passed[:2], wide_y[1], wide_y[2], *passed[2:])
    wide_z = (wide_z[0], send_z(up_z, 1), send_z(down_z, -1))
    wide_y = (wide_y[0], send_y(up_y, 1), send_y(down_y, -1))

    d_res, d_qkv_second, send_f, keep_f = call(
        functools.partial(second_back_kernel, factor=factor),
        [((288, 512), BF), ((288, 1536), BF), ((256, 2048), BF), ((256, 2048), BF)],
        [
            ((576, 512), BF),
            ((576, 512), BF),
            ((288, 512), BF),
            ((576, 512), BF),
            ((576, 1536), BF),
            ((512, 576), BF),
            ((512, 576), BF),
        ],
        scalars=1,
        us=10,
        after=(up_z,),
    )(
        place,
        d_last,
        d_tail,
        d_first,
        d_qkv_first,
        x_first,
        x_second,
        ctx_first,
        ctx_second,
        qkv_second,
        prob_second,
        fine_out,
    )
    *wide_first, wide_last, send_f = call(
        wide_sum_kernel,
        [((16, 3072), BF)] * 4 + [((4, 16, 3072), BF)],
        us=2,
        through=(send_f,),
    )(*wide_z, *wide_y)
    got_f = send_core(send_f)
    d_x_last, d_x_tail = call(last_back_kernel, [((144, 512), BF)] * 2, us=2)(
        d_res, d_qkv_second, x_second, fine_qkv
    )
    d_x_tail = send_lon(d_x_tail, 1, 0)
    to_z = call(joint_split_kernel, [((16, 11264), BF)] * 4, us=1, after=(d_x_last,))(
        wide_last, blocks(keep_f), blocks(got_f)
    )
    from_z = [to_z[0]] + [send_z(to_z[d], d) for d in (1, 2, 3)]
    from_y = [wide_first[0]] + [send_y(wide_first[d], d) for d in (1, 2, 3)]
    d_tokens, placed = call(place_result_kernel, [((576, 512), BF), ((8, 128), F32)], us=2)(
        d_x_first, d_x_last, d_x_tail, *result
    )
    fine, wide_keep, wide_send = call(
        joint_sum_kernel,
        [((16, 4, 2048), BF)] + [((8, 6144), BF)] * 2,
        scalars=1,
        after=(placed,),
    )(place, *from_z, *from_y)
    wide_got = send_x_lo(wide_send)
    fine = lax.all_to_all(fine, ("lon", "lat"), 0, 0, axis_index_groups=groups(), tiled=True)
    shares = call(
        shares_kernel,
        [
            ((4, 1536), F32),
            ((4, 512), F32),
            ((16, 1024), F32),
            ((8, 3072), F32),
            ((8, 1024), F32),
        ],
    )(fine, wide_keep, wide_got)
    return (
        coarse.reshape(4, 12, 3, 1024),
        d_tokens.reshape(4, 6, 24, 512).transpose(0, 2, 1, 3),
        *shares,
    )


def solution(mesh):
    grid_spec = P(None, "lon", "lat", None)
    rows_spec = P(("lon", "lat"), None)
    return jax.shard_map(
        local,
        mesh=mesh,
        in_specs=(grid_spec, grid_spec, P(), P(), P(), P(), P()),
        out_specs=(grid_spec, grid_spec) + (rows_spec,) * 5,
        check_vma=False,
    )
```
